256 devices in a mesh: context: 32 (over z_hi, x, core), tensor: 8 (over z_lo, y).
Axes of the slice: x: 4, y: 4, z: 8 (z_hi: 4, z_lo: 2; z = z_hi * 2 + z_lo), core: 2. Of those that a mesh axis runs over, the one named last changes fastest.
Arguments:
- grad_out: bfloat16 [4096, 8192], P('context'), may hold values from -6 to 6
- out_weight: bfloat16 [8192, 8192], P('tensor', 'context'), may hold values from -0.0625 to 0.0625
- query_proj: bfloat16 [4096, 8192], P('context', 'tensor'), may hold values from -6 to 6
- key_proj: bfloat16 [4096, 8192], P('context', 'tensor'), may hold values from -6 to 6
- value_proj: bfloat16 [4096, 8192], P('context', 'tensor'), may hold values from -6 to 6
- filter_taps: bfloat16 [4096, 8192], P('context', 'tensor')
- skip_gain: float32 [8192], P('tensor'), may hold values from 0.5 to 1.5
Outputs:
- grad_query: bfloat16 [4096, 8192], P('context', 'tensor')
- grad_key: bfloat16 [4096, 8192], P('context', 'tensor')
- grad_value: bfloat16 [4096, 8192], P('context', 'tensor')
- grad_filter: bfloat16 [4096, 8192], P('context', 'tensor')
- grad_weight: bfloat16 [8192, 8192], P('tensor', 'context')
The draws below stay inside these ranges and needn't reach their ends.
All inputs are finite; a program needn't handle non-finite values.
Results may differ from the reference program's by a relative error of at most 0.0049.
Values may be sent and summed in bfloat16 or wider, within the bound.
No kernel may reach another device: no remote copies, remote signals or barrier semaphores. Data moves between devices by JAX's collectives and lax.ppermute only.
A program may use at most 128 MiB of HBM per device.

```python
import math
import jax
import jax.numpy as jnp
from jax import lax

D = 8192
SEQ = 4096


def draw_filter_taps(key, part):
    key = jax.random.fold_in(key, 7)
    rate_key, noise_key = jax.random.split(key)
    low_rate = min(2.0 / SEQ, 1.0 / 40.0)
    rates = jnp.exp(jax.random.uniform(rate_key, (D,), jnp.float32, math.log(low_rate), math.log(1.0 / 30.0)))
    places = jnp.arange(SEQ, dtype=jnp.float32)
    noise = jnp.clip(jax.random.normal(noise_key, (SEQ, D), jnp.float32), -6.0, 6.0)
    taps = jnp.sqrt(2.0 * rates * SEQ)[None, :] * jnp.exp(-rates[None, :] * places[:, None]) * noise
    return taps.astype(jnp.bfloat16)


def raised(drawn, own_key, source, target, parts, factor):
    owner, partner = [(jnp.arange(drawn.shape[axis_at]) // (drawn.shape[axis_at] // parts)).reshape([-1 if axis == axis_at else 1 for axis in range(drawn.ndim)]) for axis_at in (source, target)]
    chosen = jax.random.permutation(own_key, parts)[partner]
    strong = (owner == chosen) | (owner == (partner + parts // 2) % parts)
    return jnp.where(strong, factor * drawn, drawn)


def block_scale(own_key, dims, shards, least, largest):
    gain = 1.0
    for position, blocks in shards:
        steps = jax.random.uniform(jax.random.fold_in(jax.random.fold_in(own_key, 6), position), (blocks,), jnp.float32, least / len(shards), largest / len(shards))
        gain = gain * jnp.repeat(jnp.exp(steps), dims[position] // blocks).reshape((-1,) + (1,) * (len(dims) - 1 - position))
    return gain


def centred(key, extent, width, limit, shards=(), kind=jnp.bfloat16):
    level = block_scale(key, extent, shards, -0.22, 0.18) if shards else 1.0
    drawn = jax.random.normal(key, extent, jnp.float32) * width * level
    return jnp.minimum(jnp.maximum(drawn, -limit), limit).astype(kind)


def heavy_noise(stream_key, dims, scale, limit, pieces, heavy, kind=jnp.bfloat16):
    values = scale * jax.random.normal(stream_key, dims, jnp.float32)
    if pieces:
        values = values * block_scale(stream_key, dims, pieces, -0.22, 0.18)
    return jnp.clip(raised(values, jax.random.fold_in(stream_key, 3), *heavy), -limit, limit).astype(kind)


def setup_inputs(seed: int = 0) -> dict:
    streams_of = jax.random.split(jax.random.key(seed), 8)
    grad_out = heavy_noise(streams_of[0], (SEQ, D), 1.0, 6.0, ((0, 32),), (1, 0, 32, 2.75))
    out_weight = centred(streams_of[1], (D, D), D ** -0.5, 0.0625, ((0, 8), (1, 32)))
    query_proj = centred(streams_of[2], (SEQ, D), 1.0, 6.0, ((0, 32), (1, 8)))
    key_proj = centred(streams_of[3], (SEQ, D), 1.0, 6.0, ((0, 32), (1, 8)))
    value_proj = centred(streams_of[4], (SEQ, D), 1.0, 6.0, ((0, 32), (1, 8)))
    filter_taps = draw_filter_taps(jax.random.fold_in(streams_of[7], 71), 0)
    skip_gain = jnp.clip(0.5 + 1.0 * jax.random.uniform(streams_of[6], (D,), jnp.float32) ** block_scale(streams_of[6], (D,), ((0, 8),), -0.2, 0.2), 0.5, 1.5)
    return dict(grad_out=grad_out, out_weight=out_weight, query_proj=query_proj, key_proj=key_proj, value_proj=value_proj, filter_taps=filter_taps, skip_gain=skip_gain)


def channel_block(items):
    mix_block, query_block, key_block, value_block, taps_block, skip_block = items
    padded_len = 2 * SEQ
    norm_scale = 1.0 / math.sqrt(SEQ)
    query_vals = query_block.astype(jnp.float32)
    key_vals = key_block.astype(jnp.float32)
    value_vals = value_block.astype(jnp.float32)
    filt = taps_block.astype(jnp.float32) * norm_scale
    gated = key_vals * value_vals

    def spectrum(field):
        return jnp.fft.rfft(field, n=padded_len, axis=0)

    def restore(spec_vals):
        return jnp.fft.irfft(spec_vals, n=padded_len, axis=0)[:SEQ]
    gated_spec = spectrum(gated)
    filt_spec = spectrum(filt)
    total = restore(filt_spec * gated_spec) + skip_block[None, :] * gated
    mixed = (query_vals * total).astype(jnp.bfloat16)
    grad_query = (mix_block * total).astype(jnp.bfloat16)
    gsig = mix_block * query_vals
    gsig_spec = spectrum(gsig)
    grad_gated = restore(jnp.conj(filt_spec) * gsig_spec) + skip_block[None, :] * gsig
    grad_taps = restore(jnp.conj(gated_spec) * gsig_spec) * norm_scale
    return (grad_query, (grad_gated * value_vals).astype(jnp.bfloat16), (grad_gated * key_vals).astype(jnp.bfloat16), grad_taps.astype(jnp.bfloat16), mixed)

def reference(grad_out, out_weight, query_proj, key_proj, value_proj, filter_taps, skip_gain):
    grad_mix = jnp.dot(grad_out, out_weight.T, preferred_element_type=jnp.float32)
    block_width = min(D, 512)
    blocks = D // block_width

    def split_cols(array):
        return array.reshape(SEQ, blocks, block_width).transpose(1, 0, 2)

    def join_cols(array):
        return array.transpose(1, 0, 2).reshape(SEQ, D)
    results = lax.map(channel_block, (split_cols(grad_mix), split_cols(query_proj), split_cols(key_proj), split_cols(value_proj), split_cols(filter_taps), skip_gain.reshape(blocks, block_width)))
    mixed = join_cols(results[4])
    grad_weight = (jnp.dot(mixed.T, grad_out, preferred_element_type=jnp.float32) * (1.0 / math.sqrt(SEQ))).astype(jnp.bfloat16)
    return (join_cols(results[0]), join_cols(results[1]), join_cols(results[2]), join_cols(results[3]), grad_weight)
```

```python
import functools
import math

import jax
import jax.numpy as jnp
import numpy as np
from jax import lax
from jax.experimental import pallas as pl
from jax.experimental.pallas import tpu as pltpu
from jax.sharding import Mesh
from jax.sharding import PartitionSpec as P

bf16 = jnp.bfloat16
f32 = jnp.float32
CTX = ("zh", "x", "core")
TEN = ("zl", "y")
VMEM_LIMIT = 48 * 1024 * 1024

OUTER, INNER = 64, 128
KEPT = OUTER // 2 + 1
HALF = OUTER // 2
GROUP = 16


def split_const(value):
    high = value.astype(np.float32).astype(bf16)
    low = (value - high.astype(np.float64)).astype(np.float32).astype(bf16)
    return np.stack([np.asarray(high), np.asarray(low)])


@functools.cache
def tables(seq_len):
    length = 2 * seq_len
    i = np.arange(HALF)
    k = np.arange(KEPT)
    turn = 2.0 * np.pi * np.outer(k, i) / OUTER
    rows = np.concatenate([np.cos(turn), -np.sin(turn)[1:HALF]], 0)
    first = split_const(np.kron(rows, np.eye(8)))
    weight = np.where((k == 0) | (k == HALF), 1.0, 2.0)[:, None]
    back = np.concatenate([weight * np.cos(turn), -(weight * np.sin(turn))[1:HALF]], 0).T
    last = split_const(np.kron(back / (length * math.sqrt(seq_len)), np.eye(8)))
    b = np.arange(INNER)
    twist = 2.0 * np.pi * np.outer(k, b) / length
    twist = np.stack([np.cos(twist), np.sin(twist)]).astype(np.float32)
    inner = 2.0 * np.pi * np.outer(b, b) / INNER
    c, s = np.cos(inner), np.sin(inner)
    ahead = split_const(np.block([[c, -s], [s, c]]))
    behind = split_const(np.block([[c, s], [-s, c]]))
    return first, twist, ahead, behind, last


def dot(a, b):
    return jnp.dot(a, b, preferred_element_type=f32)


def split(x):
    high = x.astype(bf16)
    return high, (x - high.astype(f32)).astype(bf16)


def forward(field, first_ref, twist_ref, ahead_ref):
    packed = jnp.concatenate(
        [field[:, 8 * g : 8 * g + 8].reshape(8 * HALF, INNER) for g in range(2)], 1
    ).astype(bf16)
    mixed = dot(first_ref[0], packed) + dot(first_ref[1], packed)
    halves = [mixed[:, INNER * g : INNER * (g + 1)].reshape(OUTER, 8, INNER) for g in range(2)]
    both = jnp.concatenate(halves, 1)
    zero = jnp.zeros((1, GROUP, INNER), f32)
    re = both[:KEPT]
    im = jnp.concatenate([zero, both[KEPT:], zero], 0)
    cos, sin = twist_ref[0][:, None, :], twist_ref[1][:, None, :]
    turned = jnp.concatenate([re * cos + im * sin, im * cos - re * sin], 2)
    high, low = split(turned.reshape(KEPT * GROUP, 2 * INNER))
    spec = dot(high, ahead_ref[0]) + (dot(low, ahead_ref[0]) + dot(high, ahead_ref[1]))
    return spec[:, :INNER], spec[:, INNER:]


def backward(re, im, twist_ref, behind_ref, last_ref):
    high, low = split(jnp.concatenate([re, im], 1))
    turned = dot(high, behind_ref[0]) + (dot(low, behind_ref[0]) + dot(high, behind_ref[1]))
    re = turned[:, :INNER].reshape(KEPT, GROUP, INNER)
    im = turned[:, INNER:].reshape(KEPT, GROUP, INNER)
    cos, sin = twist_ref[0][:, None, :], twist_ref[1][:, None, :]
    rows = jnp.concatenate([re * cos - im * sin, (re * sin + im * cos)[1:HALF]], 0)
    packed = jnp.concatenate(
        [rows[:, 8 * g : 8 * g + 8].reshape(8 * OUTER, INNER) for g in range(2)], 1
    )
    high, low = split(packed)
    field = dot(last_ref[0], high) + (dot(last_ref[0], low) + dot(last_ref[1], high))
    return jnp.concatenate(
        [field[:, INNER * g : INNER * (g + 1)].reshape(HALF, 8, INNER) for g in range(2)], 1
    )


def conv_kernel(
    fields_ref, skip_ref, first_ref, twist_ref, ahead_ref, behind_ref, last_ref, total_ref, spec_ref
):
    gated = fields_ref[:, 0].astype(f32)
    taps = fields_ref[:, 1].astype(f32)
    gated_re, gated_im = forward(gated, first_ref, twist_ref, ahead_ref)
    taps_re, taps_im = forward(taps, first_ref, twist_ref, ahead_ref)
    for place, part in enumerate((gated_re, gated_im, taps_re, taps_im)):
        spec_ref[place, 0] = part
    conv = backward(
        taps_re * gated_re - taps_im * gated_im,
        taps_re * gated_im + taps_im * gated_re,
        twist_ref,
        behind_ref,
        last_ref,
    )
    total_ref[...] = (conv + skip_ref[...][None] * gated).astype(bf16)


def corr_kernel(
    gsig_ref, spec_ref, skip_ref, first_ref, twist_ref, ahead_ref, behind_ref, last_ref, out_ref
):
    gsig = gsig_ref[...].astype(f32)
    gsig_re, gsig_im = forward(gsig, first_ref, twist_ref, ahead_ref)
    gated_re, gated_im, taps_re, taps_im = [spec_ref[place, 0] for place in range(4)]
    grad_gated = backward(
        taps_re * gsig_re + taps_im * gsig_im,
        taps_re * gsig_im - taps_im * gsig_re,
        twist_ref,
        behind_ref,
        last_ref,
    )
    out_ref[:, 0] = (grad_gated + skip_ref[...][None] * gsig).astype(bf16)
    grad_taps = backward(
        gated_re * gsig_re + gated_im * gsig_im,
        gated_re * gsig_im - gated_im * gsig_re,
        twist_ref,
        behind_ref,
        last_ref,
    )
    out_ref[:, 1] = grad_taps.astype(bf16)


def whole(array):
    rank = array.ndim
    return pl.BlockSpec(array.shape, lambda g: (0,) * rank)


def conv_call(fields, skip_rows, consts):
    blocks, _, owned, inner = fields.shape
    steps = owned // GROUP
    spec_rows = KEPT * GROUP
    return pl.pallas_call(
        conv_kernel,
        grid=(steps,),
        in_specs=[
            pl.BlockSpec((blocks, 2, GROUP, inner), lambda g: (0, 0, g, 0)),
            pl.BlockSpec((GROUP, inner), lambda g: (g, 0)),
        ]
        + [whole(item) for item in consts],
        out_specs=[
            pl.BlockSpec((blocks, GROUP, inner), lambda g: (0, g, 0)),
            pl.BlockSpec((4, 1, spec_rows, inner), lambda g: (0, g, 0, 0)),
        ],
        out_shape=[
            jax.ShapeDtypeStruct((blocks, owned, inner), bf16),
            jax.ShapeDtypeStruct((4, steps, spec_rows, inner), f32),
        ],
        compiler_params=pltpu.CompilerParams(vmem_limit_bytes=VMEM_LIMIT),
        cost_estimate=pl.CostEstimate(flops=10**9, bytes_accessed=6 * 2**20, transcendentals=0),
        name="conv",
    )(fields, skip_rows, *consts)


def corr_call(gsig, spec, skip_rows, consts):
    blocks, owned, inner = gsig.shape
    steps = owned // GROUP
    spec_rows = KEPT * GROUP
    return pl.pallas_call(
        corr_kernel,
        grid=(steps,),
        in_specs=[
            pl.BlockSpec((blocks, GROUP, inner), lambda g: (0, g, 0)),
            pl.BlockSpec((4, 1, spec_rows, inner), lambda g: (0, g, 0, 0)),
            pl.BlockSpec((GROUP, inner), lambda g: (g, 0)),
        ]
        + [whole(item) for item in consts],
        out_specs=pl.BlockSpec((blocks, 2, GROUP, inner), lambda g: (0, 0, g, 0)),
        out_shape=jax.ShapeDtypeStruct((blocks, 2, owned, inner), bf16),
        compiler_params=pltpu.CompilerParams(vmem_limit_bytes=VMEM_LIMIT),
        cost_estimate=pl.CostEstimate(flops=10**9, bytes_accessed=6 * 2**20, transcendentals=0),
        name="corr",
    )(gsig, spec, skip_rows, *consts)


def pick_kernel(place_ref, in_ref, out_ref):
    out_ref[0] = in_ref[...]


def pick_blocks(grad_out, places, width):
    rows = grad_out.shape[0]
    count = places.shape[0]
    return pl.pallas_call(
        pick_kernel,
        grid_spec=pltpu.PrefetchScalarGridSpec(
            num_scalar_prefetch=1,
            grid=(count,),
            in_specs=[pl.BlockSpec((rows, width), lambda n, place_ref: (0, place_ref[n]))],
            out_specs=pl.BlockSpec((1, rows, width), lambda n, place_ref: (n, 0, 0)),
        ),
        out_shape=jax.ShapeDtypeStruct((count, rows, width), grad_out.dtype),
        cost_estimate=pl.CostEstimate(flops=0, bytes_accessed=2**20, transcendentals=0),
        name="pick",
    )(places, grad_out)


def mix_kernel(*refs):
    weights, grads, outs = refs[:8], refs[8:12], refs[12:]
    step = 256
    for pair in range(2):
        lines = [
            jnp.concatenate([grads[2 * pair + n][r] for r in range(8)], 1) for n in range(2)
        ]
        grad = jnp.concatenate(lines, 0)

        def body(m, _, grad=grad, pair=pair):
            here = pl.ds(pl.multiple_of(m * step, step), step)
            weight = jnp.concatenate([w[here, :] for w in weights], 1)
            part = lax.dot_general(
                weight, grad, (((1,), (1,)), ((), ())), preferred_element_type=f32
            )
            for n in range(2):
                out = outs[2 * pair + n]
                out[here, :] = part[:, INNER * n : INNER * (n + 1)].astype(out.dtype)
            return 0

        lax.fori_loop(0, weights[0].shape[0] // step, body, 0)


def mix_call(weights, grads):
    rows = weights[0].shape[0]
    toks = grads[0].shape[1]
    kinds = (f32, bf16, bf16, bf16)
    return pl.pallas_call(
        mix_kernel,
        out_shape=[jax.ShapeDtypeStruct((rows, toks), kind) for kind in kinds],
        compiler_params=pltpu.CompilerParams(vmem_limit_bytes=VMEM_LIMIT),
        cost_estimate=pl.CostEstimate(
            flops=2 * rows * toks * 4 * 2048, bytes_accessed=8 * 2**20, transcendentals=0
        ),
        name="mix",
    )(*weights, *grads)


def ring(size, shift):
    return [(n, (n + shift) % size) for n in range(size)]


def shards(grad_out, out_weight, query_proj, key_proj, value_proj, filter_taps, skip_gain):
    tok_rows = grad_out.shape[0]
    context_size = lax.axis_size(CTX)
    size_z, size_x = lax.axis_size("zh"), lax.axis_size("x")
    seq_len = tok_rows * context_size
    group_width, width = out_weight.shape
    owned = group_width // context_size
    norm_scale = 1.0 / math.sqrt(seq_len)
    my_z, my_x, my_core = (lax.axis_index(name) for name in CTX)
    consts = [jnp.asarray(item) for item in tables(seq_len)]

    def swap(item):
        return lax.ppermute(item, "core", [(0, 1), (1, 0)])

    def shift_z(item, by):
        return lax.ppermute(item, "zh", ring(size_z, by % size_z)) if by % size_z else item

    def shift_x(item, by):
        return lax.ppermute(item, "x", ring(size_x, by % size_x)) if by % size_x else item

    def to_all(item):
        return lax.all_to_all(item, CTX, split_axis=0, concat_axis=0, tiled=True)

    gated = (key_proj.astype(f32) * value_proj.astype(f32)).astype(bf16)
    fields = jnp.stack(
        [
            gated.T.reshape(context_size, owned, tok_rows),
            filter_taps.T.reshape(context_size, owned, tok_rows),
        ],
        1,
    )
    fields = to_all(fields)

    order = (0, 1, 3, 2)
    grads = {}
    for s in order:
        places = jnp.stack(
            [
                ((my_z - r) % size_z * size_x + (my_x + s) % size_x) * 2 + (my_core + rc) % 2
                for rc in range(2)
                for r in range(size_z)
            ]
        ).astype(jnp.int32)
        grads[s] = shift_x(pick_blocks(grad_out, places, width), s)
    weights = {r: shift_z(out_weight, r) for r in order}
    weights_far = {r: swap(weights[r]) for r in order}

    skip_rows = lax.dynamic_slice_in_dim(
        skip_gain, lax.axis_index(CTX) * owned, owned, 0
    )
    skip_rows = jnp.broadcast_to(skip_rows[:, None], (owned, tok_rows))
    total, spec = conv_call(fields, skip_rows, consts)
    total = to_all(total).reshape(group_width, tok_rows)
    query_t = query_proj.T
    mixed = (query_t.astype(f32) * total.astype(f32)).astype(bf16)

    parts = mix_call(
        [weights[r] for r in range(size_z)] + [weights_far[r] for r in range(size_z)],
        [grads[s] for s in range(size_x)],
    )
    grad_mix = parts[0]
    for s in order[1:]:
        grad_mix = grad_mix + shift_x(parts[s], -s).astype(f32)
    gsig = (grad_mix * query_t.astype(f32)).astype(bf16)
    grad_query = (grad_mix * total.astype(f32)).astype(bf16).T
    gsig = to_all(gsig.reshape(context_size, owned, tok_rows))
    corr = to_all(corr_call(gsig, spec, skip_rows, consts))
    grad_gated = corr[:, 0].reshape(group_width, tok_rows).T
    grad_filter = corr[:, 1].reshape(group_width, tok_rows).T
    grad_key = (grad_gated.astype(f32) * value_proj.astype(f32)).astype(bf16)
    grad_value = (grad_gated.astype(f32) * key_proj.astype(f32)).astype(bf16)

    lines = [shift_x(mixed, s) for s in range(size_x)]
    lines = jnp.concatenate(lines, 1)
    lines = jnp.concatenate([lines, swap(lines)], 1)
    far = [swap(grads[s][size_z:]) for s in range(size_x)]
    grad_weight = None
    for r in order[::-1]:
        columns = jnp.concatenate(
            [grads[s][r] for s in range(size_x)] + [far[s][r] for s in range(size_x)], 0
        )
        product = dot(lines, columns)
        if r:
            product = shift_z(product.astype(bf16), -r).astype(f32)
        grad_weight = product if grad_weight is None else grad_weight + product
    grad_weight = (grad_weight * norm_scale).astype(bf16)
    return (grad_query, grad_key, grad_value, grad_filter, grad_weight)


def solution(mesh):
    fine = Mesh(mesh.devices.reshape(4, 4, 2, 2, 4), CTX + TEN)
    rows_cols = P(CTX, TEN)
    in_specs = (P(CTX, None), P(TEN, CTX)) + (rows_cols,) * 4 + (P(TEN),)
    out_specs = (rows_cols,) * 4 + (P(TEN, CTX),)
    return jax.shard_map(
        shards, mesh=fine, in_specs=in_specs, out_specs=out_specs, check_vma=False
    )
```

```python
import functools
import math

import jax
import jax.numpy as jnp
import numpy as np
from jax import lax
from jax.experimental import pallas as pl
from jax.experimental.pallas import tpu as pltpu
from jax.sharding import Mesh
from jax.sharding import PartitionSpec as P

bf16 = jnp.bfloat16
f32 = jnp.float32
CTX = ("zh", "x", "core")
TEN = ("zl", "y")
VMEM_LIMIT = 60 * 1024 * 1024

OUTER, INNER = 64, 128
KEPT = OUTER // 2 + 1
HALF = OUTER // 2
GROUP = 16


@functools.cache
def tables(seq_len):
    length = 2 * seq_len
    i = np.arange(HALF)
    k = np.arange(KEPT)
    turn = 2.0 * np.pi * np.outer(k, i) / OUTER
    rows = np.concatenate([np.cos(turn), -np.sin(turn)[1:HALF]], 0)
    first = np.repeat(rows, 8, axis=1)
    weight = np.where((k == 0) | (k == HALF), 1.0, 2.0)[:, None]
    back = np.concatenate([weight * np.cos(turn), -(weight * np.sin(turn))[1:HALF]], 0).T
    last = np.repeat(back / (length * math.sqrt(seq_len)), 8, axis=1)
    b = np.arange(INNER)
    inner = 2.0 * np.pi * np.outer(b, b) / INNER
    twist = 2.0 * np.pi * np.outer(k, b) / length
    pieces = [first[:, :INNER], first[:, INNER:]]
    pieces += [last[:, INNER * n : INNER * (n + 1)] for n in range(4)]
    pieces += [np.cos(inner), np.sin(inner), np.cos(twist), np.sin(twist)]
    pieces = [np.pad(item, ((0, -len(item) % 8), (0, 0))) for item in pieces]
    return np.concatenate(pieces).astype(np.float32)


def unpack(table_ref):
    places = [0]
    for size in (OUTER, OUTER) + (HALF,) * 4 + (INNER, INNER, KEPT + 7, KEPT + 7):
        places.append(places[-1] + size)
    first_a, first_b, *back, c, s, cos, sin = [
        table_ref[places[n] : places[n + 1]] for n in range(10)
    ]

    def spread(table):
        rows, cols = table.shape
        shape = (rows, 8, cols)
        own = lax.broadcasted_iota(jnp.int32, shape, 1) == (
            lax.broadcasted_iota(jnp.int32, shape, 2) & 7
        )
        wide = jnp.broadcast_to(table[:, None, :], shape)
        return jnp.where(own, wide, 0.0).reshape(rows * 8, cols)

    first = split(spread(jnp.concatenate([first_a, first_b], 1)))
    last = split(spread(jnp.concatenate(back, 1)))
    ahead = split(jnp.concatenate([jnp.concatenate([c, -s], 1), jnp.concatenate([s, c], 1)], 0))
    behind = split(jnp.concatenate([jnp.concatenate([c, s], 1), jnp.concatenate([-s, c], 1)], 0))
    return first, (cos[:KEPT], sin[:KEPT]), ahead, behind, last


def dot(a, b):
    return jnp.dot(a, b, preferred_element_type=f32)


def split(x):
    high = x.astype(bf16)
    return high, (x - high.astype(f32)).astype(bf16)


def forward(field, first, twist, ahead, exact=True):
    packed = jnp.concatenate(
        [field[:, 8 * g : 8 * g + 8].reshape(8 * HALF, INNER) for g in range(2)], 1
    )
    high, low = split(packed)
    mixed = dot(first[0], high) + dot(first[1], high)
    if not exact:
        mixed = mixed + dot(first[0], low)
    halves = [mixed[:, INNER * g : INNER * (g + 1)].reshape(OUTER, 8, INNER) for g in range(2)]
    both = jnp.concatenate(halves, 1)
    zero = jnp.zeros((1, GROUP, INNER), f32)
    re = both[:KEPT]
    im = jnp.concatenate([zero, both[KEPT:], zero], 0)
    cos, sin = twist[0][:, None, :], twist[1][:, None, :]
    turned = jnp.concatenate([re * cos + im * sin, im * cos - re * sin], 2)
    high, low = split(turned.reshape(KEPT * GROUP, 2 * INNER))
    spec = dot(high, ahead[0]) + (dot(low, ahead[0]) + dot(high, ahead[1]))
    return spec[:, :INNER], spec[:, INNER:]


def backward(re, im, twist, behind, last):
    high, low = split(jnp.concatenate([re, im], 1))
    turned = dot(high, behind[0]) + (dot(low, behind[0]) + dot(high, behind[1]))
    re = turned[:, :INNER].reshape(KEPT, GROUP, INNER)
    im = turned[:, INNER:].reshape(KEPT, GROUP, INNER)
    cos, sin = twist[0][:, None, :], twist[1][:, None, :]
    rows = jnp.concatenate([re * cos - im * sin, (re * sin + im * cos)[1:HALF]], 0)
    packed = jnp.concatenate(
        [rows[:, 8 * g : 8 * g + 8].reshape(8 * OUTER, INNER) for g in range(2)], 1
    )
    high, low = split(packed)
    field = dot(last[0], high) + (dot(last[0], low) + dot(last[1], high))
    return jnp.concatenate(
        [field[:, INNER * g : INNER * (g + 1)].reshape(HALF, 8, INNER) for g in range(2)], 1
    )


def conv_kernel(place_ref, fields_ref, skip_ref, table_ref, *refs):
    total_ref, spec_ref, *mixed_refs, hold_ref = refs[-7:]
    first, twist, ahead, behind, last = unpack(table_ref)
    gated = fields_ref[:, 0].astype(f32)
    taps = fields_ref[:, 1].astype(f32)
    gated_re, gated_im = forward(gated, first, twist, ahead)
    taps_re, taps_im = forward(taps, first, twist, ahead)
    for place, part in enumerate((gated_re, gated_im, taps_re, taps_im)):
        spec_ref[place, 0] = part
    conv = backward(
        taps_re * gated_re - taps_im * gated_im,
        taps_re * gated_im + taps_im * gated_re,
        twist,
        behind,
        last,
    )
    total = conv + skip_ref[...][None] * gated
    total_ref[...] = total
    hold_ref[...] = (total * fields_ref[:, 2].astype(f32)).astype(bf16)
    for s, mixed_ref in enumerate(mixed_refs):
        x = lax.rem(place_ref[1] + s, 4)
        for core in range(2):
            for z in range(4):
                place = (core * 4 + z) * INNER
                mixed_ref[:, place : place + INNER] = hold_ref[z * 8 + x * 2 + core]


def corr_kernel(parts_ref, fields_ref, total_ref, spec_ref, skip_ref, table_ref, *refs):
    out_ref = refs[-1]
    first, twist, ahead, behind, last = unpack(table_ref)
    grad_mix = []
    for z in range(4):
        here = slice(z * INNER, (z + 1) * INNER)
        terms = [parts_ref[8 * n : 8 * n + 8, :, here].astype(f32) for n in range(4)]
        grad_mix.append((terms[0] + terms[1]) + (terms[2] + terms[3]))
    grad_mix = jnp.concatenate(grad_mix, 0)
    out_ref[:, 2] = (grad_mix * total_ref[...]).astype(bf16)
    gsig = grad_mix * fields_ref[:, 0].astype(f32)
    gsig_re, gsig_im = forward(gsig, first, twist, ahead, exact=False)
    gated_re, gated_im, taps_re, taps_im = [spec_ref[place, 0] for place in range(4)]
    grad_gated = backward(
        taps_re * gsig_re + taps_im * gsig_im,
        taps_re * gsig_im - taps_im * gsig_re,
        twist,
        behind,
        last,
    )
    out_ref[:, 0] = (grad_gated + skip_ref[...][None] * gsig).astype(bf16)
    grad_taps = backward(
        gated_re * gsig_re + gated_im * gsig_im,
        gated_re * gsig_im - gated_im * gsig_re,
        twist,
        behind,
        last,
    )
    out_ref[:, 1] = grad_taps.astype(bf16)


def params():
    return pltpu.CompilerParams(vmem_limit_bytes=VMEM_LIMIT)


def cost(flops, megabytes):
    return pl.CostEstimate(flops=flops, bytes_accessed=megabytes * 2**20, transcendentals=0)


def conv_call(place, fields, skip_rows, table, after):
    blocks, _, owned, inner = fields.shape
    steps = owned // GROUP
    spec_rows = KEPT * GROUP
    return pl.pallas_call(
        conv_kernel,
        grid=(steps,),
        in_specs=[
            pl.BlockSpec(memory_space=pltpu.SMEM),
            pl.BlockSpec((blocks, 3, GROUP, inner), lambda g: (0, 0, g, 0)),
            pl.BlockSpec((GROUP, inner), lambda g: (g, 0)),
            pl.BlockSpec(table.shape, lambda g: (0, 0)),
        ]
        + [pl.BlockSpec(memory_space=pl.ANY)] * len(after),
        out_specs=[
            pl.BlockSpec((blocks, GROUP, inner), lambda g: (0, g, 0)),
            pl.BlockSpec((4, 1, spec_rows, inner), lambda g: (0, g, 0, 0)),
        ]
        + [pl.BlockSpec((GROUP, 8 * inner), lambda g: (g, 0))] * 4,
        out_shape=[
            jax.ShapeDtypeStruct((blocks, owned, inner), f32),
            jax.ShapeDtypeStruct((4, steps, spec_rows, inner), f32),
        ]
        + [jax.ShapeDtypeStruct((owned, 8 * inner), bf16)] * 4,
        scratch_shapes=[pltpu.VMEM((blocks, GROUP, inner), bf16)],
        compiler_params=params(),
        cost_estimate=cost(10**9, 6),
        name="conv",
    )(place, fields, skip_rows, table, *after)


def corr_call(parts, fields, total, spec, skip_rows, table, after):
    blocks, owned, inner = total.shape
    steps = owned // GROUP
    spec_rows = KEPT * GROUP
    return pl.pallas_call(
        corr_kernel,
        grid=(steps,),
        in_specs=[
            pl.BlockSpec((blocks, GROUP, 4 * inner), lambda g: (0, g, 0)),
            pl.BlockSpec((blocks, 1, GROUP, inner), lambda g: (0, 2, g, 0)),
            pl.BlockSpec((blocks, GROUP, inner), lambda g: (0, g, 0)),
            pl.BlockSpec((4, 1, spec_rows, inner), lambda g: (0, g, 0, 0)),
            pl.BlockSpec((GROUP, inner), lambda g: (g, 0)),
            pl.BlockSpec(table.shape, lambda g: (0, 0)),
        ]
        + [pl.BlockSpec(memory_space=pl.ANY)] * len(after),
        out_specs=pl.BlockSpec((blocks, 3, GROUP, inner), lambda g: (0, 0, g, 0)),
        out_shape=jax.ShapeDtypeStruct((blocks, 3, owned, inner), bf16),
        compiler_params=params(),
        cost_estimate=cost(10**9, 6),
        name="corr",
    )(parts, fields, total, spec, skip_rows, table, *after)


def prep_kernel(key_ref, value_ref, taps_ref, query_ref, *refs):
    fields_ref = refs[-1]
    gated = key_ref[...].astype(f32) * value_ref[...].astype(f32)
    shape = fields_ref.shape[:1] + fields_ref.shape[2:]
    fields_ref[:, 0] = gated.T.astype(bf16).reshape(shape)
    fields_ref[:, 1] = taps_ref[...].astype(f32).T.astype(bf16).reshape(shape)
    fields_ref[:, 2] = query_ref[...].astype(f32).T.astype(bf16).reshape(shape)


def prep_call(key_proj, value_proj, filter_taps, query_proj, owned, after):
    toks, channels = key_proj.shape
    wide = 512
    tall = pl.BlockSpec((toks, wide), lambda n: (0, n))
    return pl.pallas_call(
        prep_kernel,
        grid=(channels // wide,),
        in_specs=[tall] * 4 + [pl.BlockSpec(memory_space=pl.ANY)] * len(after),
        out_specs=pl.BlockSpec((wide // owned, 3, owned, toks), lambda n: (n, 0, 0, 0)),
        out_shape=jax.ShapeDtypeStruct((channels // owned, 3, owned, toks), bf16),
        compiler_params=params(),
        cost_estimate=cost(10**7, 2),
        name="prep",
    )(key_proj, value_proj, filter_taps, query_proj, *after)


def last_kernel(corr_ref, key_ref, value_ref, grad_key_ref, grad_value_ref, grad_filter_ref, grad_query_ref):
    rows = corr_ref.shape[0] * corr_ref.shape[2]

    def turned(n):
        return corr_ref[:, n].astype(f32).reshape(rows, corr_ref.shape[3]).T

    grad_gated = turned(0)
    grad_key_ref[...] = (grad_gated * value_ref[...].astype(f32)).astype(bf16)
    grad_value_ref[...] = (grad_gated * key_ref[...].astype(f32)).astype(bf16)
    grad_filter_ref[...] = turned(1).astype(bf16)
    grad_query_ref[...] = turned(2).astype(bf16)


def last_call(corr, key_proj, value_proj):
    toks, channels = key_proj.shape
    owned = corr.shape[2]
    wide = 512
    tall = pl.BlockSpec((toks, wide), lambda n: (0, n))
    return pl.pallas_call(
        last_kernel,
        grid=(channels // wide,),
        in_specs=[pl.BlockSpec((wide // owned, 3, owned, toks), lambda n: (n, 0, 0, 0)), tall, tall],
        out_specs=[tall] * 4,
        out_shape=[jax.ShapeDtypeStruct((toks, channels), bf16)] * 4,
        compiler_params=params(),
        cost_estimate=cost(10**7, 3),
        name="last",
    )(corr, key_proj, value_proj)


def mix_kernel(place_ref, grad_out_ref, *refs):
    near_w, far_w, passed = refs[:4], refs[4:8], refs[8:12]
    parts, near_out, far_out = refs[13:16]
    weight, grad, sems, out_sems = refs[16:]
    my_z, my_x, my_core, my_y = (place_ref[n] for n in range(4))
    width = weight.shape[3]
    copies = []

    def begin(source, target):
        copy = pltpu.make_async_copy(source, target, sems.at[len(copies)])
        copy.start()
        copies.append(copy)

    for back in range(4):
        col = lax.rem(my_x - back + 4, 4)
        begin(near_w[back], weight.at[my_core, col])
        begin(far_w[back], weight.at[1 - my_core, col])
    for back in range(4):
        for core in range(2):
            for s in range(1, 4):
                begin(
                    passed[back].at[s - 1, :, pl.ds(core * width, width)],
                    grad.at[lax.rem(my_y - back + 4, 4), core, lax.rem(my_z - s + 4, 4)],
                )
    for col in range(4):
        for core in range(2):
            start = pl.multiple_of(((my_z * 4 + col) * 2 + core) * width, width)
            begin(grad_out_ref.at[:, pl.ds(start, width)], grad.at[col, core, my_z])
    for copy in copies:
        copy.wait()

    near_copy = pltpu.make_async_copy(grad.at[:, my_core], near_out, out_sems.at[0])
    far_copy = pltpu.make_async_copy(grad.at[:, 1 - my_core], far_out, out_sems.at[1])
    near_copy.start()
    far_copy.start()

    step = 256
    for pair in ((0, 1), (2, 3)):
        lines = [jnp.concatenate([grad[n // 2, n % 2, z] for n in range(8)], 1) for z in pair]
        grad_rows = jnp.concatenate(lines, 0)
        toks = grad_rows.shape[0]

        def body(m, _, grad_rows=grad_rows, pair=pair, toks=toks):
            here = pl.ds(pl.multiple_of(m * step, step), step)
            rows = jnp.concatenate([weight[n % 2, n // 2, here, :] for n in range(8)], 1)
            part = lax.dot_general(
                rows, grad_rows, (((1,), (1,)), ((), ())), preferred_element_type=f32
            )
            start = pair[0] // 2 * toks
            parts[here, start : start + toks] = part.astype(bf16)
            return 0

        lax.fori_loop(0, weight.shape[2] // step, body, 0)
    near_copy.wait()
    far_copy.wait()


def mix_call(place, grad_out, near_w, far_w, passed, after):
    toks = grad_out.shape[0]
    rows, width = near_w[0].shape
    any_spec = pl.BlockSpec(memory_space=pl.ANY)
    vmem = pl.BlockSpec(memory_space=pltpu.VMEM)
    blocks = jax.ShapeDtypeStruct((4, 4, toks, width), bf16)
    return pl.pallas_call(
        mix_kernel,
        in_specs=[pl.BlockSpec(memory_space=pltpu.SMEM)] + [any_spec] * 14,
        out_specs=[vmem] + [any_spec] * 2,
        out_shape=[jax.ShapeDtypeStruct((rows, 4 * toks), bf16)] + [blocks] * 2,
        scratch_shapes=[
            pltpu.VMEM((2, 4, rows, width), bf16),
            pltpu.VMEM((4, 2, 4, toks, width), bf16),
            pltpu.SemaphoreType.DMA((40,)),
            pltpu.SemaphoreType.DMA((2,)),
        ],
        compiler_params=params(),
        cost_estimate=cost(2 * rows * toks * 4 * 8 * width, 9),
        name="mix",
    )(place, grad_out, *near_w, *far_w, *passed, after)


def product_kernel(cols_ref, *refs):
    mixed, near, far, outs = refs[:8], refs[8], refs[9], refs[11:]
    my_z, my_core = cols_ref[4], cols_ref[5]
    my_x = cols_ref[6]
    xs, owned, depth = mixed[0].shape
    half = depth // 2
    lines = [
        jnp.concatenate([mixed[4 * n + s][...].reshape(xs * owned, depth) for s in range(4)], 0)
        for n in range(2)
    ]
    for n, out in enumerate(outs):
        col = cols_ref[n]
        own = near[col].reshape(half, near.shape[3])
        other = far[col].reshape(half, far.shape[3])
        columns = jnp.concatenate(
            [jnp.where(my_core == 0, own, other), jnp.where(my_core == 0, other, own)], 0
        )
        for core, rows in zip((my_core, 1 - my_core), lines):
            product = dot(rows, columns).astype(out.dtype).reshape(4, xs, owned, near.shape[3])
            for s in range(4):
                for t in range(4):
                    z, x = lax.rem(my_z - s + 4, 4), lax.rem(my_x - t + 4, 4)
                    out[z, x, core] = product[s, t]


def product_call(cols, mixed, near, far, after, kinds):
    xs, owned, depth = mixed[0].shape
    width = near.shape[3]
    vmem = pl.BlockSpec(memory_space=pltpu.VMEM)
    return pl.pallas_call(
        product_kernel,
        in_specs=[pl.BlockSpec(memory_space=pltpu.SMEM)]
        + [vmem] * 10
        + [pl.BlockSpec(memory_space=pl.ANY)],
        out_specs=[vmem] * len(kinds),
        out_shape=[jax.ShapeDtypeStruct((4, xs, 2, owned, width), kind) for kind in kinds],
        compiler_params=params(),
        cost_estimate=cost(16 * xs * owned * width * depth * len(kinds), 5),
        name="product",
    )(cols, *mixed, near, far, after)


def shards(grad_out, out_weight, query_proj, key_proj, value_proj, filter_taps, skip_gain):
    tok_rows = grad_out.shape[0]
    context_size = lax.axis_size(CTX)
    seq_len = tok_rows * context_size
    group_width, width = out_weight.shape
    owned = group_width // context_size
    norm_scale = 1.0 / math.sqrt(seq_len)
    my_z, my_x, my_core, my_y = (lax.axis_index(name) for name in ("zh", "x", "core", "y"))
    table = jnp.asarray(tables(seq_len))
    order = (1, 3, 2)

    def shift(item, axis, by):
        size = lax.axis_size(axis)
        return lax.ppermute(item, axis, [(n, (n + by) % size) for n in range(size)])

    def swap(item):
        return shift(item, "core", 1)

    def to_all(item):
        return lax.all_to_all(item, CTX, split_axis=0, concat_axis=0, tiled=True)

    passed, near_w = {}, {0: out_weight}
    for s in order:
        start = ((my_z + s) % 4 * 4 + my_y) * (2 * width)
        passed[s] = shift(lax.dynamic_slice_in_dim(grad_out, start, 2 * width, 1), "zh", s)
        if s != 2:
            near_w[s] = shift(out_weight, "x", s)
    passed = {0: jnp.stack([passed[s] for s in range(1, 4)])}
    late_w = lax.optimization_barrier((out_weight, passed[0]))[0]
    near_w[2] = shift(late_w, "x", 2)
    for s in order:
        passed[s] = shift(passed[0], "y", s)
    held = lax.optimization_barrier((*near_w.values(), *passed.values()))
    far_w = {s: swap(item) for s, item in zip(near_w, held)}
    far_w = [far_w[s] for s in range(4)]

    fields = prep_call(key_proj, value_proj, filter_taps, query_proj, owned, [near_w[1], near_w[3], passed[0]])
    fields = to_all(fields)

    place = jnp.stack([my_z, my_x, my_core, my_y]).astype(jnp.int32)
    skip_rows = lax.dynamic_slice_in_dim(
        skip_gain, lax.axis_index(CTX) * owned, owned, 0
    )
    skip_rows = jnp.broadcast_to(skip_rows[:, None], (owned, tok_rows))
    total, spec, *mixed = conv_call(place, fields, skip_rows, table, [])
    mixed = jnp.stack(mixed[:1] + [shift(mixed[s], "x", s) for s in range(1, 4)])

    parts, near, far = mix_call(
        place, grad_out, [near_w[s] for s in range(4)], far_w, [passed[s] for s in range(4)], total
    )
    mixed = lax.optimization_barrier((mixed, parts))[0]
    far = swap(far)
    parts = to_all(parts.reshape(context_size, owned, 4 * tok_rows))

    mixed = [mixed] + [shift(mixed, "zh", s) for s in range(1, 4)]
    corr = corr_call(parts, fields, total, spec, skip_rows, table, [mixed[s] for s in order])
    mixed += [swap(item) for item in mixed]

    cols = [(my_x + s) % 4 for s in (2, 1, 3, 0)]
    near_cols = jnp.stack(cols + [my_z, my_core, my_x]).astype(jnp.int32)
    last_cols = jnp.stack(cols[3:] * 4 + [my_z, my_core, my_x]).astype(jnp.int32)
    sent = product_call(near_cols, mixed, near, far, corr, (bf16,) * 3)
    sent = {s: shift(item, "x", s) for s, item in zip((2, 1, 3), sent)}
    grad_weight = product_call(last_cols, mixed, near, far, corr, (f32,))[0]
    corr = to_all(corr)
    grad_key, grad_value, grad_filter, grad_query = last_call(corr, key_proj, value_proj)
    for s in (1, 3, 2):
        grad_weight = grad_weight + sent[s].astype(f32)
    grad_weight = (grad_weight * norm_scale).astype(bf16).reshape(group_width, width)
    return (grad_query, grad_key, grad_value, grad_filter, grad_weight)


def solution(mesh):
    fine = Mesh(mesh.devices.reshape(4, 4, 2, 2, 4), CTX + TEN)
    rows_cols = P(CTX, TEN)
    in_specs = (P(CTX, None), P(TEN, CTX)) + (rows_cols,) * 4 + (P(TEN),)
    out_specs = (rows_cols,) * 4 + (P(TEN, CTX),)
    return jax.shard_map(
        shards, mesh=fine, in_specs=in_specs, out_specs=out_specs, check_vma=False
    )
```

```python
import functools
import math

import jax
import jax.numpy as jnp
import numpy as np
from jax import lax
from jax.experimental import pallas as pl
from jax.experimental.pallas import tpu as pltpu
from jax.sharding import Mesh
from jax.sharding import PartitionSpec as P

bf16 = jnp.bfloat16
f32 = jnp.float32
CTX = ("zh", "x", "core")
TEN = ("zl", "y")
VMEM_LIMIT = 60 * 1024 * 1024

OUTER, INNER = 64, 128
KEPT = OUTER // 2 + 1
HALF = OUTER // 2
GROUP = 16


@functools.cache
def tables(seq_len):
    length = 2 * seq_len
    i = np.arange(HALF)
    k = np.arange(KEPT)
    turn = 2.0 * np.pi * np.outer(k, i) / OUTER
    rows = np.concatenate([np.cos(turn), -np.sin(turn)[1:HALF]], 0)
    first = np.repeat(rows, 8, axis=1)
    weight = np.where((k == 0) | (k == HALF), 1.0, 2.0)[:, None]
    back = np.concatenate([weight * np.cos(turn), -(weight * np.sin(turn))[1:HALF]], 0).T
    last = np.repeat(back / (length * math.sqrt(seq_len)), 8, axis=1)
    b = np.arange(INNER)
    inner = 2.0 * np.pi * np.outer(b, b) / INNER
    twist = 2.0 * np.pi * np.outer(k, b) / length
    pieces = [first[:, :INNER], first[:, INNER:]]
    pieces += [last[:, INNER * n : INNER * (n + 1)] for n in range(4)]
    pieces += [np.cos(inner), np.sin(inner), np.cos(twist), np.sin(twist)]
    pieces = [np.pad(item, ((0, -len(item) % 8), (0, 0))) for item in pieces]
    return np.concatenate(pieces).astype(np.float32)


def unpack(table_ref):
    places = [0]
    for size in (OUTER, OUTER) + (HALF,) * 4 + (INNER, INNER, KEPT + 7, KEPT + 7):
        places.append(places[-1] + size)
    first_a, first_b, *back, c, s, cos, sin = [
        table_ref[places[n] : places[n + 1]] for n in range(10)
    ]

    def spread(table):
        rows, cols = table.shape
        shape = (rows, 8, cols)
        own = lax.broadcasted_iota(jnp.int32, shape, 1) == (
            lax.broadcasted_iota(jnp.int32, shape, 2) & 7
        )
        wide = jnp.broadcast_to(table[:, None, :], shape)
        return jnp.where(own, wide, 0.0).reshape(rows * 8, cols)

    first = split(spread(jnp.concatenate([first_a, first_b], 1)))
    last = split(spread(jnp.concatenate(back, 1)))
    ahead = split(jnp.concatenate([jnp.concatenate([c, -s], 1), jnp.concatenate([s, c], 1)], 0))
    behind = split(jnp.concatenate([jnp.concatenate([c, s], 1), jnp.concatenate([-s, c], 1)], 0))
    return first, (cos[:KEPT], sin[:KEPT]), ahead, behind, last


def dot(a, b):
    return jnp.dot(a, b, preferred_element_type=f32)


def split(x):
    high = x.astype(bf16)
    return high, (x - high.astype(f32)).astype(bf16)


def forward(field, first, twist, ahead, exact=True):
    packed = jnp.concatenate(
        [field[:, 8 * g : 8 * g + 8].reshape(8 * HALF, INNER) for g in range(2)], 1
    )
    high, low = split(packed)
    mixed = dot(first[0], high) + dot(first[1], high)
    if not exact:
        mixed = mixed + dot(first[0], low)
    halves = [mixed[:, INNER * g : INNER * (g + 1)].reshape(OUTER, 8, INNER) for g in range(2)]
    both = jnp.concatenate(halves, 1)
    zero = jnp.zeros((1, GROUP, INNER), f32)
    re = both[:KEPT]
    im = jnp.concatenate([zero, both[KEPT:], zero], 0)
    cos, sin = twist[0][:, None, :], twist[1][:, None, :]
    turned = jnp.concatenate([re * cos + im * sin, im * cos - re * sin], 2)
    high, low = split(turned.reshape(KEPT * GROUP, 2 * INNER))
    spec = dot(high, ahead[0]) + (dot(low, ahead[0]) + dot(high, ahead[1]))
    return spec[:, :INNER], spec[:, INNER:]


def backward(re, im, twist, behind, last):
    high, low = split(jnp.concatenate([re, im], 1))
    turned = dot(high, behind[0]) + (dot(low, behind[0]) + dot(high, behind[1]))
    re = turned[:, :INNER].reshape(KEPT, GROUP, INNER)
    im = turned[:, INNER:].reshape(KEPT, GROUP, INNER)
    cos, sin = twist[0][:, None, :], twist[1][:, None, :]
    rows = jnp.concatenate([re * cos - im * sin, (re * sin + im * cos)[1:HALF]], 0)
    packed = jnp.concatenate(
        [rows[:, 8 * g : 8 * g + 8].reshape(8 * OUTER, INNER) for g in range(2)], 1
    )
    high, low = split(packed)
    field = dot(last[0], high) + (dot(last[0], low) + dot(last[1], high))
    return jnp.concatenate(
        [field[:, INNER * g : INNER * (g + 1)].reshape(HALF, 8, INNER) for g in range(2)], 1
    )


def conv_kernel(fields_ref, skip_ref, table_ref, *refs):
    total_ref, spec_ref, mixed_ref = refs[-3:]
    first, twist, ahead, behind, last = unpack(table_ref)
    gated = fields_ref[:, 0].astype(f32)
    taps = fields_ref[:, 1].astype(f32)
    gated_re, gated_im = forward(gated, first, twist, ahead)
    taps_re, taps_im = forward(taps, first, twist, ahead)
    for place, part in enumerate((gated_re, gated_im, taps_re, taps_im)):
        spec_ref[place, 0] = part
    conv = backward(
        taps_re * gated_re - taps_im * gated_im,
        taps_re * gated_im + taps_im * gated_re,
        twist,
        behind,
        last,
    )
    total = conv + skip_ref[...][None] * gated
    total_ref[...] = total
    mixed = (total * fields_ref[:, 2].astype(f32)).astype(bf16)
    for x in range(4):
        for core in range(2):
            for z in range(4):
                place = (core * 4 + z) * INNER
                block = mixed[z * 8 + x * 2 + core]
                for copy in range(4):
                    mixed_ref[copy, x, :, place : place + INNER] = block


def corr_kernel(parts_ref, fields_ref, total_ref, spec_ref, skip_ref, table_ref, *refs):
    out_ref = refs[-1]
    first, twist, ahead, behind, last = unpack(table_ref)
    grad_mix = []
    for z in range(4):
        here = slice(z * INNER, (z + 1) * INNER)
        terms = [parts_ref[8 * n : 8 * n + 8, :, here].astype(f32) for n in range(4)]
        grad_mix.append((terms[0] + terms[1]) + (terms[2] + terms[3]))
    grad_mix = jnp.concatenate(grad_mix, 0)
    out_ref[:, 2] = (grad_mix * total_ref[...]).astype(bf16)
    gsig = grad_mix * fields_ref[:, 0].astype(f32)
    gsig_re, gsig_im = forward(gsig, first, twist, ahead, exact=False)
    gated_re, gated_im, taps_re, taps_im = [spec_ref[place, 0] for place in range(4)]
    grad_gated = backward(
        taps_re * gsig_re + taps_im * gsig_im,
        taps_re * gsig_im - taps_im * gsig_re,
        twist,
        behind,
        last,
    )
    out_ref[:, 0] = (grad_gated + skip_ref[...][None] * gsig).astype(bf16)
    grad_taps = backward(
        gated_re * gsig_re + gated_im * gsig_im,
        gated_re * gsig_im - gated_im * gsig_re,
        twist,
        behind,
        last,
    )
    out_ref[:, 1] = grad_taps.astype(bf16)


def params():
    return pltpu.CompilerParams(vmem_limit_bytes=VMEM_LIMIT)


def cost(flops, megabytes):
    return pl.CostEstimate(flops=flops, bytes_accessed=megabytes * 2**20, transcendentals=0)


def conv_call(fields, skip_rows, table, after):
    blocks, _, owned, inner = fields.shape
    steps = owned // GROUP
    spec_rows = KEPT * GROUP
    return pl.pallas_call(
        conv_kernel,
        grid=(steps,),
        in_specs=[
            pl.BlockSpec((blocks, 3, GROUP, inner), lambda g: (0, 0, g, 0)),
            pl.BlockSpec((GROUP, inner), lambda g: (g, 0)),
            pl.BlockSpec(table.shape, lambda g: (0, 0)),
        ]
        + [pl.BlockSpec(memory_space=pl.ANY)] * len(after),
        out_specs=[
            pl.BlockSpec((blocks, GROUP, inner), lambda g: (0, g, 0)),
            pl.BlockSpec((4, 1, spec_rows, inner), lambda g: (0, g, 0, 0)),
            pl.BlockSpec((4, 4, GROUP, 8 * inner), lambda g: (0, 0, g, 0)),
        ],
        out_shape=[
            jax.ShapeDtypeStruct((blocks, owned, inner), f32),
            jax.ShapeDtypeStruct((4, steps, spec_rows, inner), f32),
            jax.ShapeDtypeStruct((4, 4, owned, 8 * inner), bf16),
        ],
        compiler_params=params(),
        cost_estimate=cost(10**9, 6),
        name="conv",
    )(fields, skip_rows, table, *after)


def corr_call(parts, fields, total, spec, skip_rows, table, after):
    blocks, owned, inner = total.shape
    steps = owned // GROUP
    spec_rows = KEPT * GROUP
    return pl.pallas_call(
        corr_kernel,
        grid=(steps,),
        in_specs=[
            pl.BlockSpec((blocks, GROUP, 4 * inner), lambda g: (0, g, 0)),
            pl.BlockSpec((blocks, 1, GROUP, inner), lambda g: (0, 2, g, 0)),
            pl.BlockSpec((blocks, GROUP, inner), lambda g: (0, g, 0)),
            pl.BlockSpec((4, 1, spec_rows, inner), lambda g: (0, g, 0, 0)),
            pl.BlockSpec((GROUP, inner), lambda g: (g, 0)),
            pl.BlockSpec(table.shape, lambda g: (0, 0)),
        ]
        + [pl.BlockSpec(memory_space=pl.ANY)] * len(after),
        out_specs=pl.BlockSpec((blocks, 3, GROUP, inner), lambda g: (0, 0, g, 0)),
        out_shape=jax.ShapeDtypeStruct((blocks, 3, owned, inner), bf16),
        compiler_params=params(),
        cost_estimate=cost(10**9, 6),
        name="corr",
    )(parts, fields, total, spec, skip_rows, table, *after)


def prep_kernel(key_ref, value_ref, taps_ref, query_ref, *refs):
    fields_ref = refs[-1]
    gated = key_ref[...].astype(f32) * value_ref[...].astype(f32)
    shape = fields_ref.shape[:1] + fields_ref.shape[2:]
    fields_ref[:, 0] = gated.T.astype(bf16).reshape(shape)
    fields_ref[:, 1] = taps_ref[...].astype(f32).T.astype(bf16).reshape(shape)
    fields_ref[:, 2] = query_ref[...].astype(f32).T.astype(bf16).reshape(shape)


def prep_call(key_proj, value_proj, filter_taps, query_proj, owned, after):
    toks, channels = key_proj.shape
    wide = 512
    tall = pl.BlockSpec((toks, wide), lambda n: (0, n))
    return pl.pallas_call(
        prep_kernel,
        grid=(channels // wide,),
        in_specs=[tall] * 4 + [pl.BlockSpec(memory_space=pl.ANY)] * len(after),
        out_specs=pl.BlockSpec((wide // owned, 3, owned, toks), lambda n: (n, 0, 0, 0)),
        out_shape=jax.ShapeDtypeStruct((channels // owned, 3, owned, toks), bf16),
        compiler_params=params(),
        cost_estimate=cost(10**7, 2),
        name="prep",
    )(key_proj, value_proj, filter_taps, query_proj, *after)


def last_kernel(corr_ref, key_ref, value_ref, grad_key_ref, grad_value_ref, grad_filter_ref, grad_query_ref):
    rows = corr_ref.shape[0] * corr_ref.shape[2]

    def turned(n):
        return corr_ref[:, n].astype(f32).reshape(rows, corr_ref.shape[3]).T

    grad_gated = turned(0)
    grad_key_ref[...] = (grad_gated * value_ref[...].astype(f32)).astype(bf16)
    grad_value_ref[...] = (grad_gated * key_ref[...].astype(f32)).astype(bf16)
    grad_filter_ref[...] = turned(1).astype(bf16)
    grad_query_ref[...] = turned(2).astype(bf16)


def last_call(corr, key_proj, value_proj):
    toks, channels = key_proj.shape
    owned = corr.shape[2]
    wide = 512
    tall = pl.BlockSpec((toks, wide), lambda n: (0, n))
    return pl.pallas_call(
        last_kernel,
        grid=(channels // wide,),
        in_specs=[pl.BlockSpec((wide // owned, 3, owned, toks), lambda n: (n, 0, 0, 0)), tall, tall],
        out_specs=[tall] * 4,
        out_shape=[jax.ShapeDtypeStruct((toks, channels), bf16)] * 4,
        compiler_params=params(),
        cost_estimate=cost(10**7, 3),
        name="last",
    )(corr, key_proj, value_proj)


def mix_kernel(place_ref, grad_out_ref, *refs):
    near_w, far_w, passed = refs[:4], refs[4:8], refs[8:12]
    parts, near_out, far_out = refs[13:16]
    weight, grad, sems, out_sems = refs[16:]
    my_z, my_x, my_core, my_y = (place_ref[n] for n in range(4))
    width = weight.shape[3]
    copies = []

    def begin(source, target):
        copy = pltpu.make_async_copy(source, target, sems.at[len(copies)])
        copy.start()
        copies.append(copy)

    for back in range(4):
        col = lax.rem(my_x - back + 4, 4)
        begin(near_w[back], weight.at[my_core, col])
        begin(far_w[back], weight.at[1 - my_core, col])
    for back in range(4):
        for core in range(2):
            for s in range(1, 4):
                begin(
                    passed[back].at[s - 1, :, pl.ds(core * width, width)],
                    grad.at[lax.rem(my_y - back + 4, 4), core, lax.rem(my_z - s + 4, 4)],
                )
    for col in range(4):
        for core in range(2):
            start = pl.multiple_of(((my_z * 4 + col) * 2 + core) * width, width)
            begin(grad_out_ref.at[:, pl.ds(start, width)], grad.at[col, core, my_z])
    for copy in copies:
        copy.wait()

    near_copy = pltpu.make_async_copy(grad.at[:, my_core], near_out, out_sems.at[0])
    far_copy = pltpu.make_async_copy(grad.at[:, 1 - my_core], far_out, out_sems.at[1])
    near_copy.start()
    far_copy.start()

    step = 256
    for pair in ((0, 1), (2, 3)):
        lines = [jnp.concatenate([grad[n // 2, n % 2, z] for n in range(8)], 1) for z in pair]
        grad_rows = jnp.concatenate(lines, 0)
        toks = grad_rows.shape[0]

        def body(m, _, grad_rows=grad_rows, pair=pair, toks=toks):
            here = pl.ds(pl.multiple_of(m * step, step), step)
            rows = jnp.concatenate([weight[n % 2, n // 2, here, :] for n in range(8)], 1)
            part = lax.dot_general(
                rows, grad_rows, (((1,), (1,)), ((), ())), preferred_element_type=f32
            )
            start = pair[0] // 2 * toks
            parts[here, start : start + toks] = part.astype(bf16)
            return 0

        lax.fori_loop(0, weight.shape[2] // step, body, 0)
    near_copy.wait()
    far_copy.wait()


def mix_call(place, grad_out, near_w, far_w, passed, after):
    toks = grad_out.shape[0]
    rows, width = near_w[0].shape
    any_spec = pl.BlockSpec(memory_space=pl.ANY)
    vmem = pl.BlockSpec(memory_space=pltpu.VMEM)
    blocks = jax.ShapeDtypeStruct((4, 4, toks, width), bf16)
    return pl.pallas_call(
        mix_kernel,
        in_specs=[pl.BlockSpec(memory_space=pltpu.SMEM)] + [any_spec] * 14,
        out_specs=[vmem] + [any_spec] * 2,
        out_shape=[jax.ShapeDtypeStruct((rows, 4 * toks), bf16)] + [blocks] * 2,
        scratch_shapes=[
            pltpu.VMEM((2, 4, rows, width), bf16),
            pltpu.VMEM((4, 2, 4, toks, width), bf16),
            pltpu.SemaphoreType.DMA((40,)),
            pltpu.SemaphoreType.DMA((2,)),
        ],
        compiler_params=params(),
        cost_estimate=cost(2 * rows * toks * 4 * 8 * width, 9),
        name="mix",
    )(place, grad_out, *near_w, *far_w, *passed, after)


def product_kernel(cols_ref, mixed_near, mixed_far, near, far, _, *outs):
    my_core = cols_ref[4]
    owners, owned, depth = mixed_near.shape
    half = depth // 2
    lines = [item[...].reshape(owners * owned, depth) for item in (mixed_near, mixed_far)]
    for n, out in enumerate(outs):
        col = cols_ref[n]
        own = near[col].reshape(half, near.shape[3])
        other = far[col].reshape(half, far.shape[3])
        columns = jnp.concatenate(
            [jnp.where(my_core == 0, own, other), jnp.where(my_core == 0, other, own)], 0
        )
        for core, rows in zip((my_core, 1 - my_core), lines):
            product = dot(rows, columns).astype(out.dtype)
            out[:, core] = product.reshape(owners, owned, product.shape[1])


def product_call(cols, mixed_near, mixed_far, near, far, after, kinds):
    owners, owned, depth = mixed_near.shape
    width = near.shape[3]
    vmem = pl.BlockSpec(memory_space=pltpu.VMEM)
    return pl.pallas_call(
        product_kernel,
        in_specs=[pl.BlockSpec(memory_space=pltpu.SMEM)] + [vmem] * 4 + [pl.BlockSpec(memory_space=pl.ANY)],
        out_specs=[vmem] * len(kinds),
        out_shape=[jax.ShapeDtypeStruct((owners, 2, owned, width), kind) for kind in kinds],
        compiler_params=params(),
        cost_estimate=cost(4 * owners * owned * width * depth * len(kinds), 5),
        name="product",
    )(cols, mixed_near, mixed_far, near, far, after)


def shards(grad_out, out_weight, query_proj, key_proj, value_proj, filter_taps, skip_gain):
    tok_rows = grad_out.shape[0]
    context_size = lax.axis_size(CTX)
    seq_len = tok_rows * context_size
    group_width, width = out_weight.shape
    owned = group_width // context_size
    norm_scale = 1.0 / math.sqrt(seq_len)
    my_z, my_x, my_core, my_y = (lax.axis_index(name) for name in ("zh", "x", "core", "y"))
    table = jnp.asarray(tables(seq_len))
    order = (1, 3, 2)

    def shift(item, axis, by):
        size = lax.axis_size(axis)
        return lax.ppermute(item, axis, [(n, (n + by) % size) for n in range(size)])

    def swap(item):
        return shift(item, "core", 1)

    def to_all(item):
        return lax.all_to_all(item, CTX, split_axis=0, concat_axis=0, tiled=True)

    passed, near_w = {}, {0: out_weight}
    for s in order:
        start = ((my_z + s) % 4 * 4 + my_y) * (2 * width)
        passed[s] = shift(lax.dynamic_slice_in_dim(grad_out, start, 2 * width, 1), "zh", s)
        if s != 2:
            near_w[s] = shift(out_weight, "x", s)
    passed = {0: jnp.stack([passed[s] for s in range(1, 4)])}
    late_w = lax.optimization_barrier((out_weight, passed[0]))[0]
    near_w[2] = shift(late_w, "x", 2)
    for s in order:
        passed[s] = shift(passed[0], "y", s)
    place = jnp.stack([my_z, my_x, my_core, my_y]).astype(jnp.int32)
    skip_rows = lax.dynamic_slice_in_dim(
        skip_gain, lax.axis_index(CTX) * owned, owned, 0
    )
    skip_rows = jnp.broadcast_to(skip_rows[:, None], (owned, tok_rows))

    fields = prep_call(key_proj, value_proj, filter_taps, query_proj, owned, [near_w[1], near_w[3], passed[0], skip_rows, place])
    fields = to_all(fields)

    total, spec, mixed = conv_call(
        fields, skip_rows, table, [near_w[2]] + [passed[s] for s in order]
    )
    mixed = lax.all_to_all(
        mixed.reshape(16, owned, 8 * tok_rows), ("zh", "x"), split_axis=0, concat_axis=0, tiled=True
    )

    held = lax.optimization_barrier((*near_w.values(), *passed.values(), total))
    far_w = {s: swap(item) for s, item in zip(near_w, held)}
    far_w = [far_w[s] for s in range(4)]
    parts, near, far = mix_call(
        place, grad_out, [near_w[s] for s in range(4)], far_w, [passed[s] for s in range(4)], total
    )
    far = swap(far)
    parts = to_all(parts.reshape(context_size, owned, 4 * tok_rows))
    mixed_far = swap(mixed)

    cols = [(my_x + s) % 4 for s in (2, 1, 3, 0)]
    near_cols = jnp.stack(cols + [my_core]).astype(jnp.int32)
    last_cols = jnp.stack(cols[3:] * 4 + [my_core]).astype(jnp.int32)
    sent = product_call(near_cols, mixed, mixed_far, near, far, total, (bf16,) * 3)
    sent = {s: shift(item, "x", s) for s, item in zip((2, 1, 3), sent)}
    corr = corr_call(parts, fields, total, spec, skip_rows, table, [sent[1], sent[3]])
    grad_weight = product_call(last_cols, mixed, mixed_far, near, far, corr, (f32,))[0]
    corr = to_all(corr)
    grad_key, grad_value, grad_filter, grad_query = last_call(corr, key_proj, value_proj)
    for s in (1, 3, 2):
        grad_weight = grad_weight + sent[s].astype(f32)
    grad_weight = (grad_weight * norm_scale).astype(bf16).reshape(group_width, width)
    return (grad_query, grad_key, grad_value, grad_filter, grad_weight)


def solution(mesh):
    fine = Mesh(mesh.devices.reshape(4, 4, 2, 2, 4), CTX + TEN)
    rows_cols = P(CTX, TEN)
    in_specs = (P(CTX, None), P(TEN, CTX)) + (rows_cols,) * 4 + (P(TEN),)
    out_specs = (rows_cols,) * 4 + (P(TEN, CTX),)
    return jax.shard_map(
        shards, mesh=fine, in_specs=in_specs, out_specs=out_specs, check_vma=False
    )
```

```python
import functools
import math

import jax
import jax.numpy as jnp
import numpy as np
from jax import lax
from jax.experimental import pallas as pl
from jax.experimental.pallas import tpu as pltpu
from jax.sharding import Mesh
from jax.sharding import PartitionSpec as P

bf16 = jnp.bfloat16
f32 = jnp.float32
CTX = ("zh", "x", "core")
TEN = ("zl", "y")
VMEM_LIMIT = 60 * 1024 * 1024

OUTER, INNER = 64, 128
KEPT = OUTER // 2 + 1
HALF = OUTER // 2
GROUP = 16


@functools.cache
def tables(seq_len):
    length = 2 * seq_len
    i = np.arange(HALF)
    k = np.arange(KEPT)
    turn = 2.0 * np.pi * np.outer(k, i) / OUTER
    rows = np.concatenate([np.cos(turn), -np.sin(turn)[1:HALF]], 0)
    first = np.repeat(rows, 8, axis=1)
    weight = np.where((k == 0) | (k == HALF), 1.0, 2.0)[:, None]
    back = np.concatenate([weight * np.cos(turn), -(weight * np.sin(turn))[1:HALF]], 0).T
    last = np.repeat(back / (length * math.sqrt(seq_len)), 8, axis=1)
    b = np.arange(INNER)
    inner = 2.0 * np.pi * np.outer(b, b) / INNER
    twist = 2.0 * np.pi * np.outer(k, b) / length
    pieces = [first[:, :INNER], first[:, INNER:]]
    pieces += [last[:, INNER * n : INNER * (n + 1)] for n in range(4)]
    pieces += [np.cos(inner), np.sin(inner), np.cos(twist), np.sin(twist)]
    pieces = [np.pad(item, ((0, -len(item) % 8), (0, 0))) for item in pieces]
    return np.concatenate(pieces).astype(np.float32)


def unpack(table_ref):
    places = [0]
    for size in (OUTER, OUTER) + (HALF,) * 4 + (INNER, INNER, KEPT + 7, KEPT + 7):
        places.append(places[-1] + size)
    first_a, first_b, *back, c, s, cos, sin = [
        table_ref[places[n] : places[n + 1]] for n in range(10)
    ]

    def spread(table):
        rows, cols = table.shape
        shape = (rows, 8, cols)
        own = lax.broadcasted_iota(jnp.int32, shape, 1) == (
            lax.broadcasted_iota(jnp.int32, shape, 2) & 7
        )
        wide = jnp.broadcast_to(table[:, None, :], shape)
        return jnp.where(own, wide, 0.0).reshape(rows * 8, cols)

    first = split(spread(jnp.concatenate([first_a, first_b], 1)))
    last = split(spread(jnp.concatenate(back, 1)))
    ahead = split(jnp.concatenate([jnp.concatenate([c, -s], 1), jnp.concatenate([s, c], 1)], 0))
    behind = split(jnp.concatenate([jnp.concatenate([c, s], 1), jnp.concatenate([-s, c], 1)], 0))
    return first, (cos[:KEPT], sin[:KEPT]), ahead, behind, last


def dot(a, b):
    return jnp.dot(a, b, preferred_element_type=f32)


def split(x):
    high = x.astype(bf16)
    return high, (x - high.astype(f32)).astype(bf16)


def forward(field, first, twist, ahead, exact=True):
    packed = jnp.concatenate(
        [field[:, 8 * g : 8 * g + 8].reshape(8 * HALF, INNER) for g in range(2)], 1
    )
    high, low = split(packed)
    mixed = dot(first[0], high) + dot(first[1], high)
    if not exact:
        mixed = mixed + dot(first[0], low)
    halves = [mixed[:, INNER * g : INNER * (g + 1)].reshape(OUTER, 8, INNER) for g in range(2)]
    both = jnp.concatenate(halves, 1)
    zero = jnp.zeros((1, GROUP, INNER), f32)
    re = both[:KEPT]
    im = jnp.concatenate([zero, both[KEPT:], zero], 0)
    cos, sin = twist[0][:, None, :], twist[1][:, None, :]
    turned = jnp.concatenate([re * cos + im * sin, im * cos - re * sin], 2)
    high, low = split(turned.reshape(KEPT * GROUP, 2 * INNER))
    spec = dot(high, ahead[0]) + (dot(low, ahead[0]) + dot(high, ahead[1]))
    return spec[:, :INNER], spec[:, INNER:]


def backward(re, im, twist, behind, last):
    high, low = split(jnp.concatenate([re, im], 1))
    turned = dot(high, behind[0]) + (dot(low, behind[0]) + dot(high, behind[1]))
    re = turned[:, :INNER].reshape(KEPT, GROUP, INNER)
    im = turned[:, INNER:].reshape(KEPT, GROUP, INNER)
    cos, sin = twist[0][:, None, :], twist[1][:, None, :]
    rows = jnp.concatenate([re * cos - im * sin, (re * sin + im * cos)[1:HALF]], 0)
    packed = jnp.concatenate(
        [rows[:, 8 * g : 8 * g + 8].reshape(8 * OUTER, INNER) for g in range(2)], 1
    )
    high, low = split(packed)
    field = dot(last[0], high) + (dot(last[0], low) + dot(last[1], high))
    return jnp.concatenate(
        [field[:, INNER * g : INNER * (g + 1)].reshape(HALF, 8, INNER) for g in range(2)], 1
    )


def conv_kernel(fields_ref, skip_ref, table_ref, total_ref, spec_ref, mixed_ref):
    first, twist, ahead, behind, last = unpack(table_ref)
    gated = fields_ref[:, 0].astype(f32)
    taps = fields_ref[:, 1].astype(f32)
    gated_re, gated_im = forward(gated, first, twist, ahead)
    taps_re, taps_im = forward(taps, first, twist, ahead)
    for place, part in enumerate((gated_re, gated_im, taps_re, taps_im)):
        spec_ref[place, 0] = part
    conv = backward(
        taps_re * gated_re - taps_im * gated_im,
        taps_re * gated_im + taps_im * gated_re,
        twist,
        behind,
        last,
    )
    total = conv + skip_ref[...][None] * gated
    total_ref[...] = total
    mixed = (total * fields_ref[:, 2].astype(f32)).astype(bf16)
    for x in range(4):
        for core in range(2):
            for z in range(4):
                place = (core * 4 + z) * INNER
                block = mixed[z * 8 + x * 2 + core]
                for copy in range(4):
                    mixed_ref[copy, x, :, place : place + INNER] = block


def corr_kernel(parts_ref, fields_ref, total_ref, spec_ref, skip_ref, table_ref, out_ref):
    first, twist, ahead, behind, last = unpack(table_ref)
    grad_mix = []
    for z in range(4):
        here = slice(z * INNER, (z + 1) * INNER)
        terms = [parts_ref[8 * n : 8 * n + 8, :, here].astype(f32) for n in range(4)]
        grad_mix.append((terms[0] + terms[1]) + (terms[2] + terms[3]))
    grad_mix = jnp.concatenate(grad_mix, 0)
    out_ref[:, 2] = (grad_mix * total_ref[...]).astype(bf16)
    gsig = grad_mix * fields_ref[:, 0].astype(f32)
    gsig_re, gsig_im = forward(gsig, first, twist, ahead, exact=False)
    gated_re, gated_im, taps_re, taps_im = [spec_ref[place, 0] for place in range(4)]
    grad_gated = backward(
        taps_re * gsig_re + taps_im * gsig_im,
        taps_re * gsig_im - taps_im * gsig_re,
        twist,
        behind,
        last,
    )
    out_ref[:, 0] = (grad_gated + skip_ref[...][None] * gsig).astype(bf16)
    grad_taps = backward(
        gated_re * gsig_re + gated_im * gsig_im,
        gated_re * gsig_im - gated_im * gsig_re,
        twist,
        behind,
        last,
    )
    out_ref[:, 1] = grad_taps.astype(bf16)


def params():
    return pltpu.CompilerParams(vmem_limit_bytes=VMEM_LIMIT)


def cost(flops, megabytes):
    return pl.CostEstimate(flops=flops, bytes_accessed=megabytes * 2**20, transcendentals=0)


def conv_call(fields, skip_rows, table):
    blocks, _, owned, inner = fields.shape
    steps = owned // GROUP
    spec_rows = KEPT * GROUP
    return pl.pallas_call(
        conv_kernel,
        grid=(steps,),
        in_specs=[
            pl.BlockSpec((blocks, 3, GROUP, inner), lambda g: (0, 0, g, 0)),
            pl.BlockSpec((GROUP, inner), lambda g: (g, 0)),
            pl.BlockSpec(table.shape, lambda g: (0, 0)),
        ],
        out_specs=[
            pl.BlockSpec((blocks, GROUP, inner), lambda g: (0, g, 0)),
            pl.BlockSpec((4, 1, spec_rows, inner), lambda g: (0, g, 0, 0)),
            pl.BlockSpec((4, 4, GROUP, 8 * inner), lambda g: (0, 0, g, 0)),
        ],
        out_shape=[
            jax.ShapeDtypeStruct((blocks, owned, inner), f32),
            jax.ShapeDtypeStruct((4, steps, spec_rows, inner), f32),
            jax.ShapeDtypeStruct((4, 4, owned, 8 * inner), bf16),
        ],
        compiler_params=params(),
        cost_estimate=cost(10**9, 6),
        name="conv",
    )(fields, skip_rows, table)


def corr_call(parts, fields, total, spec, skip_rows, table):
    blocks, owned, inner = total.shape
    steps = owned // GROUP
    spec_rows = KEPT * GROUP
    return pl.pallas_call(
        corr_kernel,
        grid=(steps,),
        in_specs=[
            pl.BlockSpec((blocks, GROUP, 4 * inner), lambda g: (0, g, 0)),
            pl.BlockSpec((blocks, 1, GROUP, inner), lambda g: (0, 2, g, 0)),
            pl.BlockSpec((blocks, GROUP, inner), lambda g: (0, g, 0)),
            pl.BlockSpec((4, 1, spec_rows, inner), lambda g: (0, g, 0, 0)),
            pl.BlockSpec((GROUP, inner), lambda g: (g, 0)),
            pl.BlockSpec(table.shape, lambda g: (0, 0)),
        ],
        out_specs=pl.BlockSpec((blocks, 3, GROUP, inner), lambda g: (0, 0, g, 0)),
        out_shape=jax.ShapeDtypeStruct((blocks, 3, owned, inner), bf16),
        compiler_params=params(),
        cost_estimate=cost(10**9, 6),
        name="corr",
    )(parts, fields, total, spec, skip_rows, table)


def prep_kernel(key_ref, value_ref, taps_ref, query_ref, *refs):
    fields_ref = refs[-1]
    gated = key_ref[...].astype(f32) * value_ref[...].astype(f32)
    shape = fields_ref.shape[:1] + fields_ref.shape[2:]
    fields_ref[:, 0] = gated.T.astype(bf16).reshape(shape)
    fields_ref[:, 1] = taps_ref[...].astype(f32).T.astype(bf16).reshape(shape)
    fields_ref[:, 2] = query_ref[...].astype(f32).T.astype(bf16).reshape(shape)


def prep_call(key_proj, value_proj, filter_taps, query_proj, owned):
    toks, channels = key_proj.shape
    wide = 512
    tall = pl.BlockSpec((toks, wide), lambda n: (0, n))
    return pl.pallas_call(
        prep_kernel,
        grid=(channels // wide,),
        in_specs=[tall] * 4,
        out_specs=pl.BlockSpec((wide // owned, 3, owned, toks), lambda n: (n, 0, 0, 0)),
        out_shape=jax.ShapeDtypeStruct((channels // owned, 3, owned, toks), bf16),
        compiler_params=params(),
        cost_estimate=cost(10**7, 2),
        name="prep",
    )(key_proj, value_proj, filter_taps, query_proj)


def last_kernel(corr_ref, key_ref, value_ref, grad_key_ref, grad_value_ref, grad_filter_ref, grad_query_ref):
    rows = corr_ref.shape[0] * corr_ref.shape[2]

    def turned(n):
        return corr_ref[:, n].astype(f32).reshape(rows, corr_ref.shape[3]).T

    grad_gated = turned(0)
    grad_key_ref[...] = (grad_gated * value_ref[...].astype(f32)).astype(bf16)
    grad_value_ref[...] = (grad_gated * key_ref[...].astype(f32)).astype(bf16)
    grad_filter_ref[...] = turned(1).astype(bf16)
    grad_query_ref[...] = turned(2).astype(bf16)


def last_call(corr, key_proj, value_proj):
    toks, channels = key_proj.shape
    owned = corr.shape[2]
    wide = 512
    tall = pl.BlockSpec((toks, wide), lambda n: (0, n))
    return pl.pallas_call(
        last_kernel,
        grid=(channels // wide,),
        in_specs=[pl.BlockSpec((wide // owned, 3, owned, toks), lambda n: (n, 0, 0, 0)), tall, tall],
        out_specs=[tall] * 4,
        out_shape=[jax.ShapeDtypeStruct((toks, channels), bf16)] * 4,
        compiler_params=params(),
        cost_estimate=cost(10**7, 3),
        name="last",
    )(corr, key_proj, value_proj)


def mix_kernel(place_ref, grad_out_ref, *refs):
    near_w, far_w, passed = refs[:4], refs[4:8], refs[8:12]
    parts, near_out, far_out, weight, grad, sems, out_sems = refs[-7:]
    my_z, my_x, my_core, my_y = (place_ref[n] for n in range(4))
    width = weight.shape[3]
    copies = []

    def begin(source, target):
        copy = pltpu.make_async_copy(source, target, sems.at[len(copies)])
        copy.start()
        copies.append(copy)

    for back in range(4):
        for core in range(2):
            for s in range(1, 4):
                begin(
                    passed[back].at[s - 1, :, pl.ds(core * width, width)],
                    grad.at[lax.rem(my_y - back + 4, 4), core, lax.rem(my_z - s + 4, 4)],
                )
    for col in range(4):
        for core in range(2):
            start = pl.multiple_of(((my_z * 4 + col) * 2 + core) * width, width)
            begin(grad_out_ref.at[:, pl.ds(start, width)], grad.at[col, core, my_z])
    fixed = len(copies)
    step = 256
    for m in range(weight.shape[2] // step):
        here = pl.ds(m * step, step)
        for back in range(4):
            col = lax.rem(my_x - back + 4, 4)
            begin(near_w[back].at[here], weight.at[my_core, col, here])
            begin(far_w[back].at[here], weight.at[1 - my_core, col, here])
    for copy in copies[:fixed]:
        copy.wait()

    near_copy = pltpu.make_async_copy(grad.at[:, my_core], near_out, out_sems.at[0])
    far_copy = pltpu.make_async_copy(grad.at[:, 1 - my_core], far_out, out_sems.at[1])
    near_copy.start()
    far_copy.start()

    lines = [
        jnp.concatenate([grad[n // 2, n % 2, z] for n in range(8)], 1) for z in range(4)
    ]
    grad_rows = jnp.concatenate(lines, 0)
    for m in range(weight.shape[2] // step):
        for copy in copies[fixed + 8 * m : fixed + 8 * m + 8]:
            copy.wait()
        here = slice(m * step, (m + 1) * step)
        rows = jnp.concatenate([weight[n % 2, n // 2, here, :] for n in range(8)], 1)
        part = lax.dot_general(
            rows, grad_rows, (((1,), (1,)), ((), ())), preferred_element_type=f32
        )
        parts[here, :] = part.astype(bf16)
    near_copy.wait()
    far_copy.wait()


def mix_call(place, grad_out, near_w, far_w, passed):
    toks = grad_out.shape[0]
    rows, width = near_w[0].shape
    any_spec = pl.BlockSpec(memory_space=pl.ANY)
    vmem = pl.BlockSpec(memory_space=pltpu.VMEM)
    blocks = jax.ShapeDtypeStruct((4, 4, toks, width), bf16)
    return pl.pallas_call(
        mix_kernel,
        in_specs=[pl.BlockSpec(memory_space=pltpu.SMEM)] + [any_spec] * 13,
        out_specs=[vmem] + [any_spec] * 2,
        out_shape=[jax.ShapeDtypeStruct((rows, 4 * toks), bf16)] + [blocks] * 2,
        scratch_shapes=[
            pltpu.VMEM((2, 4, rows, width), bf16),
            pltpu.VMEM((4, 2, 4, toks, width), bf16),
            pltpu.SemaphoreType.DMA((64,)),
            pltpu.SemaphoreType.DMA((2,)),
        ],
        compiler_params=params(),
        cost_estimate=cost(2 * rows * toks * 4 * 8 * width, 9),
        name="mix",
    )(place, grad_out, *near_w, *far_w, *passed)


def product_kernel(cols_ref, mixed_near, mixed_far, near, far, *outs):
    my_core = cols_ref[4]
    owners, owned, depth = mixed_near.shape
    half = depth // 2
    lines = [item[...].reshape(owners * owned, depth) for item in (mixed_near, mixed_far)]
    for n, out in enumerate(outs):
        col = cols_ref[n]
        own = near[col].reshape(half, near.shape[3])
        other = far[col].reshape(half, far.shape[3])
        columns = jnp.concatenate(
            [jnp.where(my_core == 0, own, other), jnp.where(my_core == 0, other, own)], 0
        )
        for core, rows in zip((my_core, 1 - my_core), lines):
            product = dot(rows, columns).astype(out.dtype)
            out[:, core] = product.reshape(owners, owned, product.shape[1])


def product_call(cols, mixed_near, mixed_far, near, far, kinds):
    owners, owned, depth = mixed_near.shape
    width = near.shape[3]
    vmem = pl.BlockSpec(memory_space=pltpu.VMEM)
    return pl.pallas_call(
        product_kernel,
        in_specs=[pl.BlockSpec(memory_space=pltpu.SMEM)] + [vmem] * 4,
        out_specs=[vmem] * len(kinds),
        out_shape=[jax.ShapeDtypeStruct((owners, 2, owned, width), kind) for kind in kinds],
        compiler_params=params(),
        cost_estimate=cost(4 * owners * owned * width * depth * len(kinds), 5),
        name="product",
    )(cols, mixed_near, mixed_far, near, far)


def shards(grad_out, out_weight, query_proj, key_proj, value_proj, filter_taps, skip_gain):
    tok_rows = grad_out.shape[0]
    context_size = lax.axis_size(CTX)
    seq_len = tok_rows * context_size
    group_width, width = out_weight.shape
    owned = group_width // context_size
    norm_scale = 1.0 / math.sqrt(seq_len)
    my_z, my_x, my_core, my_y = (lax.axis_index(name) for name in ("zh", "x", "core", "y"))
    table = jnp.asarray(tables(seq_len))
    order = (1, 3, 2)

    def shift(item, axis, by):
        size = lax.axis_size(axis)
        return lax.ppermute(item, axis, [(n, (n + by) % size) for n in range(size)])

    def swap(item):
        return shift(item, "core", 1)

    def to_all(item):
        return lax.all_to_all(item, CTX, split_axis=0, concat_axis=0, tiled=True)

    place = jnp.stack([my_z, my_x, my_core, my_y]).astype(jnp.int32)
    skip_rows = lax.dynamic_slice_in_dim(
        skip_gain, lax.axis_index(CTX) * owned, owned, 0
    )
    skip_rows = jnp.broadcast_to(skip_rows[:, None], (owned, tok_rows))

    def after(item, *others):
        return lax.optimization_barrier((item, *others))[0]

    packed = prep_call(key_proj, value_proj, filter_taps, query_proj, owned)
    fields = to_all(packed)
    grad_late, weight_late = after(grad_out, packed), after(out_weight, packed)

    passed, near_w = {}, {0: weight_late}
    for s in order:
        start = ((my_z + s) % 4 * 4 + my_y) * (2 * width)
        passed[s] = shift(lax.dynamic_slice_in_dim(grad_late, start, 2 * width, 1), "zh", s)
        if s != 2:
            near_w[s] = shift(weight_late, "x", s)
    passed = {0: jnp.stack([passed[s] for s in range(1, 4)])}
    near_w[2] = shift(after(out_weight, passed[0]), "x", 2)
    for s in order:
        passed[s] = shift(passed[0], "y", s)

    fields = after(fields, passed[0], near_w[1], near_w[3], skip_rows, place)
    total, spec, mixed = conv_call(fields, skip_rows, table)
    mixed = lax.all_to_all(
        mixed.reshape(16, owned, 8 * tok_rows), ("zh", "x"), split_axis=0, concat_axis=0, tiled=True
    )

    held = lax.optimization_barrier((*near_w.values(), *passed.values(), total))
    far_w = {s: swap(item) for s, item in zip(near_w, held)}
    far_w = [far_w[s] for s in range(4)]
    parts, near, far = mix_call(
        place, grad_out, [near_w[s] for s in range(4)], far_w, [passed[s] for s in range(4)]
    )
    far = swap(far)
    parts = to_all(parts.reshape(context_size, owned, 4 * tok_rows))
    mixed_far = swap(mixed)

    cols = [(my_x + s) % 4 for s in (2, 1, 3, 0)]
    near_cols = jnp.stack(cols + [my_core]).astype(jnp.int32)
    last_cols = jnp.stack(cols[3:] * 4 + [my_core]).astype(jnp.int32)
    sent = product_call(near_cols, mixed, mixed_far, near, far, (bf16,) * 3)
    sent = {s: shift(item, "x", s) for s, item in zip((2, 1, 3), sent)}
    parts = after(parts, sent[1], sent[3])
    corr = corr_call(parts, fields, total, spec, skip_rows, table)
    grad_weight = product_call(after(last_cols, corr), mixed, mixed_far, near, far, (f32,))[0]
    corr = to_all(corr)
    grad_key, grad_value, grad_filter, grad_query = last_call(corr, key_proj, value_proj)
    for s in (1, 3, 2):
        grad_weight = grad_weight + sent[s].astype(f32)
    grad_weight = (grad_weight * norm_scale).astype(bf16).reshape(group_width, width)
    return (grad_query, grad_key, grad_value, grad_filter, grad_weight)


def solution(mesh):
    fine = Mesh(mesh.devices.reshape(4, 4, 2, 2, 4), CTX + TEN)
    rows_cols = P(CTX, TEN)
    in_specs = (P(CTX, None), P(TEN, CTX)) + (rows_cols,) * 4 + (P(TEN),)
    out_specs = (rows_cols,) * 4 + (P(TEN, CTX),)
    return jax.shard_map(
        shards, mesh=fine, in_specs=in_specs, out_specs=out_specs, check_vma=False
    )
```

```python
import functools
import math

import jax
import jax.numpy as jnp
import numpy as np
from jax import lax
from jax.experimental import pallas as pl
from jax.experimental.pallas import tpu as pltpu
from jax.sharding import Mesh
from jax.sharding import PartitionSpec as P

bf16 = jnp.bfloat16
f32 = jnp.float32
CTX = ("zh", "x", "core")
TEN = ("zl", "y")
VMEM_LIMIT = 127 * 512 * 1024

OUTER, INNER = 64, 128
KEPT = OUTER // 2 + 1
HALF = OUTER // 2
GROUP = 16


@functools.cache
def tables(seq_len):
    length = 2 * seq_len
    i = np.arange(HALF)
    k = np.arange(KEPT)
    turn = 2.0 * np.pi * np.outer(k, i) / OUTER
    rows = np.concatenate([np.cos(turn), -np.sin(turn)[1:HALF]], 0)
    first = np.repeat(rows, 8, axis=1)
    weight = np.where((k == 0) | (k == HALF), 1.0, 2.0)[:, None]
    back = np.concatenate([weight * np.cos(turn), -(weight * np.sin(turn))[1:HALF]], 0).T
    last = np.repeat(back / (length * math.sqrt(seq_len)), 8, axis=1)
    b = np.arange(INNER)
    inner = 2.0 * np.pi * np.outer(b, b) / INNER
    twist = 2.0 * np.pi * np.outer(k, b) / length
    pieces = [first[:, :INNER], first[:, INNER:]]
    pieces += [last[:, INNER * n : INNER * (n + 1)] for n in range(4)]
    pieces += [np.cos(inner), np.sin(inner), np.cos(twist), np.sin(twist)]
    pieces = [np.pad(item, ((0, -len(item) % 8), (0, 0))) for item in pieces]
    return np.concatenate(pieces).astype(np.float32)


def unpack(table_ref):
    places = [0]
    for size in (OUTER, OUTER) + (HALF,) * 4 + (INNER, INNER, KEPT + 7, KEPT + 7):
        places.append(places[-1] + size)
    first_a, first_b, *back, c, s, cos, sin = [
        table_ref[places[n] : places[n + 1]] for n in range(10)
    ]

    def spread(table):
        rows, cols = table.shape
        shape = (rows, 8, cols)
        own = lax.broadcasted_iota(jnp.int32, shape, 1) == (
            lax.broadcasted_iota(jnp.int32, shape, 2) & 7
        )
        wide = jnp.broadcast_to(table[:, None, :], shape)
        return jnp.where(own, wide, 0.0).reshape(rows * 8, cols)

    first = split(spread(jnp.concatenate([first_a, first_b], 1)))
    last = split(spread(jnp.concatenate(back, 1)))
    ahead = split(jnp.concatenate([jnp.concatenate([c, -s], 1), jnp.concatenate([s, c], 1)], 0))
    behind = split(jnp.concatenate([jnp.concatenate([c, s], 1), jnp.concatenate([-s, c], 1)], 0))
    return first, (cos[:KEPT], sin[:KEPT]), ahead, behind, last


def dot(a, b):
    return jnp.dot(a, b, preferred_element_type=f32)


def split(x):
    high = x.astype(bf16)
    return high, (x - high.astype(f32)).astype(bf16)


def forward(field, first, twist, ahead, exact=True):
    packed = jnp.concatenate(
        [field[:, 8 * g : 8 * g + 8].reshape(8 * HALF, INNER) for g in range(2)], 1
    )
    high, low = split(packed)
    mixed = dot(first[0], high) + dot(first[1], high)
    if not exact:
        mixed = mixed + dot(first[0], low)
    halves = [mixed[:, INNER * g : INNER * (g + 1)].reshape(OUTER, 8, INNER) for g in range(2)]
    both = jnp.concatenate(halves, 1)
    zero = jnp.zeros((1, GROUP, INNER), f32)
    re = both[:KEPT]
    im = jnp.concatenate([zero, both[KEPT:], zero], 0)
    cos, sin = twist[0][:, None, :], twist[1][:, None, :]
    turned = jnp.concatenate([re * cos + im * sin, im * cos - re * sin], 2)
    high, low = split(turned.reshape(KEPT * GROUP, 2 * INNER))
    spec = dot(high, ahead[0]) + (dot(low, ahead[0]) + dot(high, ahead[1]))
    return spec[:, :INNER], spec[:, INNER:]


def backward(re, im, twist, behind, last):
    high, low = split(jnp.concatenate([re, im], 1))
    turned = dot(high, behind[0]) + (dot(low, behind[0]) + dot(high, behind[1]))
    re = turned[:, :INNER].reshape(KEPT, GROUP, INNER)
    im = turned[:, INNER:].reshape(KEPT, GROUP, INNER)
    cos, sin = twist[0][:, None, :], twist[1][:, None, :]
    rows = jnp.concatenate([re * cos - im * sin, (re * sin + im * cos)[1:HALF]], 0)
    packed = jnp.concatenate(
        [rows[:, 8 * g : 8 * g + 8].reshape(8 * OUTER, INNER) for g in range(2)], 1
    )
    high, low = split(packed)
    field = dot(last[0], high) + (dot(last[0], low) + dot(last[1], high))
    return jnp.concatenate(
        [field[:, INNER * g : INNER * (g + 1)].reshape(HALF, 8, INNER) for g in range(2)], 1
    )


def conv_kernel(fields_ref, skip_ref, table_ref, total_ref, spec_ref, mixed_ref):
    first, twist, ahead, behind, last = unpack(table_ref)
    gated = fields_ref[:, 0].astype(f32)
    taps = fields_ref[:, 1].astype(f32)
    gated_re, gated_im = forward(gated, first, twist, ahead)
    taps_re, taps_im = forward(taps, first, twist, ahead)
    for place, part in enumerate((gated_re, gated_im, taps_re, taps_im)):
        spec_ref[place, 0] = part
    conv = backward(
        taps_re * gated_re - taps_im * gated_im,
        taps_re * gated_im + taps_im * gated_re,
        twist,
        behind,
        last,
    )
    total = conv + skip_ref[...][None] * gated
    total_ref[...] = total
    mixed = (total * fields_ref[:, 2].astype(f32)).astype(bf16)
    for x in range(4):
        for core in range(2):
            for z in range(4):
                place = (core * 4 + z) * INNER
                block = mixed[z * 8 + x * 2 + core]
                for copy in range(4):
                    mixed_ref[copy, x, :, place : place + INNER] = block


def corr_kernel(parts_ref, fields_ref, total_ref, spec_ref, skip_ref, table_ref, out_ref):
    first, twist, ahead, behind, last = unpack(table_ref)
    grad_mix = []
    for z in range(4):
        here = slice(z * INNER, (z + 1) * INNER)
        terms = [parts_ref[8 * n : 8 * n + 8, :, here].astype(f32) for n in range(4)]
        grad_mix.append((terms[0] + terms[1]) + (terms[2] + terms[3]))
    grad_mix = jnp.concatenate(grad_mix, 0)
    out_ref[:, 2] = (grad_mix * total_ref[...]).astype(bf16)
    gsig = grad_mix * fields_ref[:, 0].astype(f32)
    gsig_re, gsig_im = forward(gsig, first, twist, ahead, exact=False)
    gated_re, gated_im, taps_re, taps_im = [spec_ref[place, 0] for place in range(4)]
    grad_gated = backward(
        taps_re * gsig_re + taps_im * gsig_im,
        taps_re * gsig_im - taps_im * gsig_re,
        twist,
        behind,
        last,
    )
    out_ref[:, 0] = (grad_gated + skip_ref[...][None] * gsig).astype(bf16)
    grad_taps = backward(
        gated_re * gsig_re + gated_im * gsig_im,
        gated_re * gsig_im - gated_im * gsig_re,
        twist,
        behind,
        last,
    )
    out_ref[:, 1] = grad_taps.astype(bf16)


def params():
    return pltpu.CompilerParams(vmem_limit_bytes=VMEM_LIMIT)


def cost(flops, megabytes):
    return pl.CostEstimate(flops=flops, bytes_accessed=megabytes * 2**20, transcendentals=0)


def conv_call(fields, skip_rows, table):
    blocks, _, owned, inner = fields.shape
    steps = owned // GROUP
    spec_rows = KEPT * GROUP
    return pl.pallas_call(
        conv_kernel,
        grid=(steps,),
        in_specs=[
            pl.BlockSpec((blocks, 3, GROUP, inner), lambda g: (0, 0, g, 0)),
            pl.BlockSpec((GROUP, inner), lambda g: (g, 0)),
            pl.BlockSpec(table.shape, lambda g: (0, 0)),
        ],
        out_specs=[
            pl.BlockSpec((blocks, GROUP, inner), lambda g: (0, g, 0)),
            pl.BlockSpec((4, 1, spec_rows, inner), lambda g: (0, g, 0, 0)),
            pl.BlockSpec((4, 4, GROUP, 8 * inner), lambda g: (0, 0, g, 0)),
        ],
        out_shape=[
            jax.ShapeDtypeStruct((blocks, owned, inner), f32),
            jax.ShapeDtypeStruct((4, steps, spec_rows, inner), f32),
            jax.ShapeDtypeStruct((4, 4, owned, 8 * inner), bf16),
        ],
        compiler_params=params(),
        cost_estimate=cost(10**9, 6),
        name="conv",
    )(fields, skip_rows, table)


def corr_call(parts, fields, total, spec, skip_rows, table):
    blocks, owned, inner = total.shape
    steps = owned // GROUP
    spec_rows = KEPT * GROUP
    return pl.pallas_call(
        corr_kernel,
        grid=(steps,),
        in_specs=[
            pl.BlockSpec((blocks, GROUP, 4 * inner), lambda g: (0, g, 0)),
            pl.BlockSpec((blocks, 1, GROUP, inner), lambda g: (0, 2, g, 0)),
            pl.BlockSpec((blocks, GROUP, inner), lambda g: (0, g, 0)),
            pl.BlockSpec((4, 1, spec_rows, inner), lambda g: (0, g, 0, 0)),
            pl.BlockSpec((GROUP, inner), lambda g: (g, 0)),
            pl.BlockSpec(table.shape, lambda g: (0, 0)),
        ],
        out_specs=pl.BlockSpec((blocks, 3, GROUP, inner), lambda g: (0, 0, g, 0)),
        out_shape=jax.ShapeDtypeStruct((blocks, 3, owned, inner), bf16),
        compiler_params=params(),
        cost_estimate=cost(10**9, 6),
        name="corr",
    )(parts, fields, total, spec, skip_rows, table)


def prep_kernel(key_ref, value_ref, taps_ref, query_ref, *refs):
    fields_ref = refs[-1]
    gated = key_ref[...].astype(f32) * value_ref[...].astype(f32)
    shape = fields_ref.shape[:1] + fields_ref.shape[2:]
    fields_ref[:, 0] = gated.T.astype(bf16).reshape(shape)
    fields_ref[:, 1] = taps_ref[...].astype(f32).T.astype(bf16).reshape(shape)
    fields_ref[:, 2] = query_ref[...].astype(f32).T.astype(bf16).reshape(shape)


def prep_call(key_proj, value_proj, filter_taps, query_proj, owned):
    toks, channels = key_proj.shape
    wide = 512
    tall = pl.BlockSpec((toks, wide), lambda n: (0, n))
    return pl.pallas_call(
        prep_kernel,
        grid=(channels // wide,),
        in_specs=[tall] * 4,
        out_specs=pl.BlockSpec((wide // owned, 3, owned, toks), lambda n: (n, 0, 0, 0)),
        out_shape=jax.ShapeDtypeStruct((channels // owned, 3, owned, toks), bf16),
        compiler_params=params(),
        cost_estimate=cost(10**7, 2),
        name="prep",
    )(key_proj, value_proj, filter_taps, query_proj)


def last_kernel(corr_ref, key_ref, value_ref, grad_key_ref, grad_value_ref, grad_filter_ref, grad_query_ref):
    rows = corr_ref.shape[0] * corr_ref.shape[2]

    def turned(n):
        return corr_ref[:, n].astype(f32).reshape(rows, corr_ref.shape[3]).T

    grad_gated = turned(0)
    grad_key_ref[...] = (grad_gated * value_ref[...].astype(f32)).astype(bf16)
    grad_value_ref[...] = (grad_gated * key_ref[...].astype(f32)).astype(bf16)
    grad_filter_ref[...] = turned(1).astype(bf16)
    grad_query_ref[...] = turned(2).astype(bf16)


def last_call(corr, key_proj, value_proj):
    toks, channels = key_proj.shape
    owned = corr.shape[2]
    wide = 512
    tall = pl.BlockSpec((toks, wide), lambda n: (0, n))
    return pl.pallas_call(
        last_kernel,
        grid=(channels // wide,),
        in_specs=[pl.BlockSpec((wide // owned, 3, owned, toks), lambda n: (n, 0, 0, 0)), tall, tall],
        out_specs=[tall] * 4,
        out_shape=[jax.ShapeDtypeStruct((toks, channels), bf16)] * 4,
        compiler_params=params(),
        cost_estimate=cost(10**7, 3),
        name="last",
    )(corr, key_proj, value_proj)


def mix_kernel(place_ref, grad_out_ref, *refs):
    near_w, far_w, passed = refs[:4], refs[4:8], refs[8:12]
    parts, near_out, far_out, weight, grad, sems, out_sems = refs[-7:]
    my_z, my_x, my_core, my_y = (place_ref[n] for n in range(4))
    width = weight.shape[3]
    copies = []

    def begin(source, target):
        copy = pltpu.make_async_copy(source, target, sems.at[len(copies)])
        copy.start()
        copies.append(copy)

    for back in range(4):
        for core in range(2):
            for s in range(1, 4):
                begin(
                    passed[back].at[s - 1, :, pl.ds(core * width, width)],
                    grad.at[lax.rem(my_y - back + 4, 4), core, lax.rem(my_z - s + 4, 4)],
                )
    for col in range(4):
        for core in range(2):
            start = pl.multiple_of(((my_z * 4 + col) * 2 + core) * width, width)
            begin(grad_out_ref.at[:, pl.ds(start, width)], grad.at[col, core, my_z])
    fixed = len(copies)
    step = 256
    for m in range(weight.shape[2] // step):
        here = pl.ds(m * step, step)
        for back in range(4):
            col = lax.rem(my_x - back + 4, 4)
            begin(near_w[back].at[here], weight.at[my_core, col, here])
            begin(far_w[back].at[here], weight.at[1 - my_core, col, here])
    for copy in copies[:fixed]:
        copy.wait()

    near_copy = pltpu.make_async_copy(grad.at[:, my_core], near_out, out_sems.at[0])
    far_copy = pltpu.make_async_copy(grad.at[:, 1 - my_core], far_out, out_sems.at[1])
    near_copy.start()
    far_copy.start()

    lines = [
        jnp.concatenate([grad[n // 2, n % 2, z] for n in range(8)], 1) for z in range(4)
    ]
    grad_rows = jnp.concatenate(lines, 0)
    for m in range(weight.shape[2] // step):
        for copy in copies[fixed + 8 * m : fixed + 8 * m + 8]:
            copy.wait()
        here = slice(m * step, (m + 1) * step)
        rows = jnp.concatenate([weight[n % 2, n // 2, here, :] for n in range(8)], 1)
        part = lax.dot_general(
            rows, grad_rows, (((1,), (1,)), ((), ())), preferred_element_type=f32
        )
        parts[here, :] = part.astype(bf16)
    near_copy.wait()
    far_copy.wait()


def mix_call(place, grad_out, near_w, far_w, passed):
    toks = grad_out.shape[0]
    rows, width = near_w[0].shape
    any_spec = pl.BlockSpec(memory_space=pl.ANY)
    vmem = pl.BlockSpec(memory_space=pltpu.VMEM)
    blocks = jax.ShapeDtypeStruct((4, 4, toks, width), bf16)
    return pl.pallas_call(
        mix_kernel,
        in_specs=[pl.BlockSpec(memory_space=pltpu.SMEM)] + [any_spec] * 13,
        out_specs=[vmem] + [any_spec] * 2,
        out_shape=[jax.ShapeDtypeStruct((rows, 4 * toks), bf16)] + [blocks] * 2,
        scratch_shapes=[
            pltpu.VMEM((2, 4, rows, width), bf16),
            pltpu.VMEM((4, 2, 4, toks, width), bf16),
            pltpu.SemaphoreType.DMA((64,)),
            pltpu.SemaphoreType.DMA((2,)),
        ],
        compiler_params=params(),
        cost_estimate=cost(2 * rows * toks * 4 * 8 * width, 9),
        name="mix",
    )(place, grad_out, *near_w, *far_w, *passed)


def product_kernel(extra, cols_ref, mixed_near, mixed_far, near, far, *refs):
    adds, outs = refs[:extra], refs[extra:]
    my_core = cols_ref[4]
    owners, owned, depth = mixed_near.shape
    half = depth // 2
    lines = [item[...].reshape(owners * owned, depth) for item in (mixed_near, mixed_far)]
    for n, out in enumerate(outs):
        col = cols_ref[n]
        own = near[col].reshape(half, near.shape[3])
        other = far[col].reshape(half, far.shape[3])
        columns = jnp.concatenate(
            [jnp.where(my_core == 0, own, other), jnp.where(my_core == 0, other, own)], 0
        )
        for core, rows in zip((my_core, 1 - my_core), lines):
            product = dot(rows, columns)
            product = product.reshape(owners, owned, product.shape[1])
            for item in adds:
                product = product + item[:, core].astype(f32)
            out[:, core] = product.astype(out.dtype)


def product_call(cols, mixed_near, mixed_far, near, far, adds, kinds):
    owners, owned, depth = mixed_near.shape
    width = near.shape[3]
    vmem = pl.BlockSpec(memory_space=pltpu.VMEM)
    return pl.pallas_call(
        functools.partial(product_kernel, len(adds)),
        in_specs=[pl.BlockSpec(memory_space=pltpu.SMEM)] + [vmem] * (4 + len(adds)),
        out_specs=[vmem] * len(kinds),
        out_shape=[jax.ShapeDtypeStruct((owners, 2, owned, width), kind) for kind in kinds],
        compiler_params=params(),
        cost_estimate=cost(4 * owners * owned * width * depth * len(kinds), 5),
        name="product",
    )(cols, mixed_near, mixed_far, near, far, *adds)


def shards(grad_out, out_weight, query_proj, key_proj, value_proj, filter_taps, skip_gain):
    tok_rows = grad_out.shape[0]
    context_size = lax.axis_size(CTX)
    seq_len = tok_rows * context_size
    group_width, width = out_weight.shape
    owned = group_width // context_size
    norm_scale = 1.0 / math.sqrt(seq_len)
    my_z, my_x, my_core, my_y = (lax.axis_index(name) for name in ("zh", "x", "core", "y"))
    table = jnp.asarray(tables(seq_len))
    order = (1, 3, 2)

    def shift(item, axis, by):
        size = lax.axis_size(axis)
        return lax.ppermute(item, axis, [(n, (n + by) % size) for n in range(size)])

    def swap(item):
        return shift(item, "core", 1)

    def to_all(item):
        return lax.all_to_all(item, CTX, split_axis=0, concat_axis=0, tiled=True)

    place = jnp.stack([my_z, my_x, my_core, my_y]).astype(jnp.int32)
    skip_rows = lax.dynamic_slice_in_dim(
        skip_gain, lax.axis_index(CTX) * owned, owned, 0
    )
    skip_rows = jnp.broadcast_to(skip_rows[:, None], (owned, tok_rows))

    def after(item, *others):
        return lax.optimization_barrier((item, *others))[0]

    packed = prep_call(key_proj, value_proj, filter_taps, query_proj, owned)
    fields = to_all(packed)
    grad_late, weight_late = after(grad_out, packed), after(out_weight, packed)

    passed, near_w = {}, {0: weight_late}
    for s in order:
        start = ((my_z + s) % 4 * 4 + my_y) * (2 * width)
        passed[s] = shift(lax.dynamic_slice_in_dim(grad_late, start, 2 * width, 1), "zh", s)
        if s != 2:
            near_w[s] = shift(weight_late, "x", s)
    passed = {0: jnp.stack([passed[s] for s in range(1, 4)])}
    near_w[2] = shift(after(out_weight, passed[0]), "x", 2)
    for s in order:
        passed[s] = shift(passed[0], "y", s)

    fields = after(fields, passed[0], near_w[1], near_w[3], skip_rows, place)
    total, spec, mixed = conv_call(fields, skip_rows, table)
    mixed = lax.all_to_all(
        mixed.reshape(16, owned, 8 * tok_rows), ("zh", "x"), split_axis=0, concat_axis=0, tiled=True
    )

    held = lax.optimization_barrier((*near_w.values(), *passed.values(), total))
    far_w = {s: swap(item) for s, item in zip(near_w, held)}
    far_w = [far_w[s] for s in range(4)]
    parts, near, far = mix_call(
        place, grad_out, [near_w[s] for s in range(4)], far_w, [passed[s] for s in range(4)]
    )
    far = swap(far)
    parts = to_all(parts.reshape(context_size, owned, 4 * tok_rows))
    mixed_far = swap(mixed)

    cols = [(my_x + s) % 4 for s in (2, 1, 3, 0)]
    near_cols = jnp.stack(cols + [my_core]).astype(jnp.int32)
    last_cols = jnp.stack(cols[3:] * 4 + [my_core]).astype(jnp.int32)
    sent = product_call(near_cols, mixed, mixed_far, near, far, (), (bf16,) * 3)
    sent = {s: shift(item, "x", s) for s, item in zip((2, 1, 3), sent)}
    parts = after(parts, sent[1], sent[3])
    corr = corr_call(parts, fields, total, spec, skip_rows, table)
    grad_weight = product_call(
        after(last_cols, corr), mixed, mixed_far, near, far, (sent[1], sent[3]), (f32,)
    )[0]
    corr = to_all(corr)
    grad_key, grad_value, grad_filter, grad_query = last_call(corr, key_proj, value_proj)
    grad_weight = grad_weight + sent[2].astype(f32)
    grad_weight = (grad_weight * norm_scale).astype(bf16).reshape(group_width, width)
    return (grad_query, grad_key, grad_value, grad_filter, grad_weight)


def solution(mesh):
    fine = Mesh(mesh.devices.reshape(4, 4, 2, 2, 4), CTX + TEN)
    rows_cols = P(CTX, TEN)
    in_specs = (P(CTX, None), P(TEN, CTX)) + (rows_cols,) * 4 + (P(TEN),)
    out_specs = (rows_cols,) * 4 + (P(TEN, CTX),)
    return jax.shard_map(
        shards, mesh=fine, in_specs=in_specs, out_specs=out_specs, check_vma=False
    )
```

```python
import functools
import math

import jax
import jax.numpy as jnp
import numpy as np
from jax import lax
from jax.experimental import pallas as pl
from jax.experimental.pallas import tpu as pltpu
from jax.sharding import Mesh
from jax.sharding import PartitionSpec as P

bf16 = jnp.bfloat16
f32 = jnp.float32
CTX = ("zh", "x", "core")
TEN = ("zl", "y")
VMEM_LIMIT = 127 * 512 * 1024

OUTER, INNER = 64, 128
KEPT = OUTER // 2 + 1
HALF = OUTER // 2
GROUP = 16


@functools.cache
def tables(seq_len):
    length = 2 * seq_len
    i = np.arange(HALF)
    k = np.arange(KEPT)
    turn = 2.0 * np.pi * np.outer(k, i) / OUTER
    rows = np.concatenate([np.cos(turn), -np.sin(turn)[1:HALF]], 0)
    first = np.repeat(rows, 8, axis=1)
    weight = np.where((k == 0) | (k == HALF), 1.0, 2.0)[:, None]
    back = np.concatenate([weight * np.cos(turn), -(weight * np.sin(turn))[1:HALF]], 0).T
    last = np.repeat(back / (length * math.sqrt(seq_len)), 8, axis=1)
    b = np.arange(INNER)
    inner = 2.0 * np.pi * np.outer(b, b) / INNER
    twist = 2.0 * np.pi * np.outer(k, b) / length
    pieces = [first[:, :INNER], first[:, INNER:]]
    pieces += [last[:, INNER * n : INNER * (n + 1)] for n in range(4)]
    pieces += [np.cos(inner), np.sin(inner), np.cos(twist), np.sin(twist)]
    pieces = [np.pad(item, ((0, -len(item) % 8), (0, 0))) for item in pieces]
    return np.concatenate(pieces).astype(np.float32)


def unpack(table_ref):
    places = [0]
    for size in (OUTER, OUTER) + (HALF,) * 4 + (INNER, INNER, KEPT + 7, KEPT + 7):
        places.append(places[-1] + size)
    first_a, first_b, *back, c, s, cos, sin = [
        table_ref[places[n] : places[n + 1]] for n in range(10)
    ]

    def spread(table):
        rows, cols = table.shape
        shape = (rows, 8, cols)
        own = lax.broadcasted_iota(jnp.int32, shape, 1) == (
            lax.broadcasted_iota(jnp.int32, shape, 2) & 7
        )
        wide = jnp.broadcast_to(table[:, None, :], shape)
        return jnp.where(own, wide, 0.0).reshape(rows * 8, cols)

    first = split(spread(jnp.concatenate([first_a, first_b], 1)))
    last = split(spread(jnp.concatenate(back, 1)))
    ahead = split(jnp.concatenate([jnp.concatenate([c, -s], 1), jnp.concatenate([s, c], 1)], 0))
    behind = split(jnp.concatenate([jnp.concatenate([c, s], 1), jnp.concatenate([-s, c], 1)], 0))
    return first, (cos[:KEPT], sin[:KEPT]), ahead, behind, last


def dot(a, b):
    return jnp.dot(a, b, preferred_element_type=f32)


def split(x):
    high = x.astype(bf16)
    return high, (x - high.astype(f32)).astype(bf16)


def forward(field, first, twist, ahead, exact=True):
    packed = jnp.concatenate(
        [field[:, 8 * g : 8 * g + 8].reshape(8 * HALF, INNER) for g in range(2)], 1
    )
    high, low = split(packed)
    mixed = dot(first[0], high) + dot(first[1], high)
    if not exact:
        mixed = mixed + dot(first[0], low)
    halves = [mixed[:, INNER * g : INNER * (g + 1)].reshape(OUTER, 8, INNER) for g in range(2)]
    both = jnp.concatenate(halves, 1)
    zero = jnp.zeros((1, GROUP, INNER), f32)
    re = both[:KEPT]
    im = jnp.concatenate([zero, both[KEPT:], zero], 0)
    cos, sin = twist[0][:, None, :], twist[1][:, None, :]
    turned = jnp.concatenate([re * cos + im * sin, im * cos - re * sin], 2)
    high, low = split(turned.reshape(KEPT * GROUP, 2 * INNER))
    spec = dot(high, ahead[0]) + (dot(low, ahead[0]) + dot(high, ahead[1]))
    return spec[:, :INNER], spec[:, INNER:]


def backward(re, im, twist, behind, last):
    high, low = split(jnp.concatenate([re, im], 1))
    turned = dot(high, behind[0]) + (dot(low, behind[0]) + dot(high, behind[1]))
    re = turned[:, :INNER].reshape(KEPT, GROUP, INNER)
    im = turned[:, INNER:].reshape(KEPT, GROUP, INNER)
    cos, sin = twist[0][:, None, :], twist[1][:, None, :]
    rows = jnp.concatenate([re * cos - im * sin, (re * sin + im * cos)[1:HALF]], 0)
    packed = jnp.concatenate(
        [rows[:, 8 * g : 8 * g + 8].reshape(8 * OUTER, INNER) for g in range(2)], 1
    )
    high, low = split(packed)
    field = dot(last[0], high) + (dot(last[0], low) + dot(last[1], high))
    return jnp.concatenate(
        [field[:, INNER * g : INNER * (g + 1)].reshape(HALF, 8, INNER) for g in range(2)], 1
    )


def conv_kernel(fields_ref, skip_ref, table_ref, total_ref, spec_ref, mixed_ref):
    first, twist, ahead, behind, last = unpack(table_ref)
    gated = fields_ref[:, 0].astype(f32)
    taps = fields_ref[:, 1].astype(f32)
    gated_re, gated_im = forward(gated, first, twist, ahead)
    taps_re, taps_im = forward(taps, first, twist, ahead)
    for place, part in enumerate((gated_re, gated_im, taps_re, taps_im)):
        spec_ref[place, 0] = part
    conv = backward(
        taps_re * gated_re - taps_im * gated_im,
        taps_re * gated_im + taps_im * gated_re,
        twist,
        behind,
        last,
    )
    total = conv + skip_ref[...][None] * gated
    total_ref[...] = total
    mixed = (total * fields_ref[:, 2].astype(f32)).astype(bf16)
    for x in range(4):
        for core in range(2):
            for z in range(4):
                place = (core * 4 + z) * INNER
                block = mixed[z * 8 + x * 2 + core]
                for copy in range(4):
                    mixed_ref[copy, x, :, place : place + INNER] = block


def corr_kernel(parts_ref, fields_ref, total_ref, spec_ref, skip_ref, table_ref, out_ref):
    first, twist, ahead, behind, last = unpack(table_ref)
    grad_mix = []
    for z in range(4):
        here = slice(z * INNER, (z + 1) * INNER)
        terms = [parts_ref[8 * n : 8 * n + 8, :, here].astype(f32) for n in range(4)]
        grad_mix.append((terms[0] + terms[1]) + (terms[2] + terms[3]))
    grad_mix = jnp.concatenate(grad_mix, 0)
    out_ref[:, 2] = (grad_mix * total_ref[...]).astype(bf16)
    gsig = grad_mix * fields_ref[:, 0].astype(f32)
    gsig_re, gsig_im = forward(gsig, first, twist, ahead, exact=False)
    gated_re, gated_im, taps_re, taps_im = [spec_ref[place, 0] for place in range(4)]
    grad_gated = backward(
        taps_re * gsig_re + taps_im * gsig_im,
        taps_re * gsig_im - taps_im * gsig_re,
        twist,
        behind,
        last,
    )
    out_ref[:, 0] = (grad_gated + skip_ref[...][None] * gsig).astype(bf16)
    grad_taps = backward(
        gated_re * gsig_re + gated_im * gsig_im,
        gated_re * gsig_im - gated_im * gsig_re,
        twist,
        behind,
        last,
    )
    out_ref[:, 1] = grad_taps.astype(bf16)


def params():
    return pltpu.CompilerParams(vmem_limit_bytes=VMEM_LIMIT)


def cost(flops, megabytes):
    return pl.CostEstimate(flops=flops, bytes_accessed=megabytes * 2**20, transcendentals=0)


def conv_call(fields, skip_rows, table):
    blocks, _, owned, inner = fields.shape
    steps = owned // GROUP
    spec_rows = KEPT * GROUP
    return pl.pallas_call(
        conv_kernel,
        grid=(steps,),
        in_specs=[
            pl.BlockSpec((blocks, 3, GROUP, inner), lambda g: (0, 0, g, 0)),
            pl.BlockSpec((GROUP, inner), lambda g: (g, 0)),
            pl.BlockSpec(table.shape, lambda g: (0, 0)),
        ],
        out_specs=[
            pl.BlockSpec((blocks, GROUP, inner), lambda g: (0, g, 0)),
            pl.BlockSpec((4, 1, spec_rows, inner), lambda g: (0, g, 0, 0)),
            pl.BlockSpec((4, 4, GROUP, 8 * inner), lambda g: (0, 0, g, 0)),
        ],
        out_shape=[
            jax.ShapeDtypeStruct((blocks, owned, inner), f32),
            jax.ShapeDtypeStruct((4, steps, spec_rows, inner), f32),
            jax.ShapeDtypeStruct((4, 4, owned, 8 * inner), bf16),
        ],
        compiler_params=params(),
        cost_estimate=cost(10**9, 6),
        name="conv",
    )(fields, skip_rows, table)


def corr_call(parts, fields, total, spec, skip_rows, table):
    blocks, owned, inner = total.shape
    steps = owned // GROUP
    spec_rows = KEPT * GROUP
    return pl.pallas_call(
        corr_kernel,
        grid=(steps,),
        in_specs=[
            pl.BlockSpec((blocks, GROUP, 4 * inner), lambda g: (0, g, 0)),
            pl.BlockSpec((blocks, 1, GROUP, inner), lambda g: (0, 2, g, 0)),
            pl.BlockSpec((blocks, GROUP, inner), lambda g: (0, g, 0)),
            pl.BlockSpec((4, 1, spec_rows, inner), lambda g: (0, g, 0, 0)),
            pl.BlockSpec((GROUP, inner), lambda g: (g, 0)),
            pl.BlockSpec(table.shape, lambda g: (0, 0)),
        ],
        out_specs=pl.BlockSpec((blocks, 3, GROUP, inner), lambda g: (0, 0, g, 0)),
        out_shape=jax.ShapeDtypeStruct((blocks, 3, owned, inner), bf16),
        compiler_params=params(),
        cost_estimate=cost(10**9, 6),
        name="corr",
    )(parts, fields, total, spec, skip_rows, table)


def prep_kernel(key_ref, value_ref, taps_ref, query_ref, *refs):
    fields_ref = refs[-1]
    gated = key_ref[...].astype(f32) * value_ref[...].astype(f32)
    shape = fields_ref.shape[:1] + fields_ref.shape[2:]
    fields_ref[:, 0] = gated.T.astype(bf16).reshape(shape)
    fields_ref[:, 1] = taps_ref[...].astype(f32).T.astype(bf16).reshape(shape)
    fields_ref[:, 2] = query_ref[...].astype(f32).T.astype(bf16).reshape(shape)


def prep_call(key_proj, value_proj, filter_taps, query_proj, owned):
    toks, channels = key_proj.shape
    wide = 512
    tall = pl.BlockSpec((toks, wide), lambda n: (0, n))
    return pl.pallas_call(
        prep_kernel,
        grid=(channels // wide,),
        in_specs=[tall] * 4,
        out_specs=pl.BlockSpec((wide // owned, 3, owned, toks), lambda n: (n, 0, 0, 0)),
        out_shape=jax.ShapeDtypeStruct((channels // owned, 3, owned, toks), bf16),
        compiler_params=params(),
        cost_estimate=cost(10**7, 2),
        name="prep",
    )(key_proj, value_proj, filter_taps, query_proj)


def last_kernel(corr_ref, key_ref, value_ref, grad_key_ref, grad_value_ref, grad_filter_ref, grad_query_ref):
    rows = corr_ref.shape[0] * corr_ref.shape[2]

    def turned(n):
        return corr_ref[:, n].astype(f32).reshape(rows, corr_ref.shape[3]).T

    grad_gated = turned(0)
    grad_key_ref[...] = (grad_gated * value_ref[...].astype(f32)).astype(bf16)
    grad_value_ref[...] = (grad_gated * key_ref[...].astype(f32)).astype(bf16)
    grad_filter_ref[...] = turned(1).astype(bf16)
    grad_query_ref[...] = turned(2).astype(bf16)


def last_call(corr, key_proj, value_proj):
    toks, channels = key_proj.shape
    owned = corr.shape[2]
    wide = 512
    tall = pl.BlockSpec((toks, wide), lambda n: (0, n))
    return pl.pallas_call(
        last_kernel,
        grid=(channels // wide,),
        in_specs=[pl.BlockSpec((wide // owned, 3, owned, toks), lambda n: (n, 0, 0, 0)), tall, tall],
        out_specs=[tall] * 4,
        out_shape=[jax.ShapeDtypeStruct((toks, channels), bf16)] * 4,
        compiler_params=params(),
        cost_estimate=cost(10**7, 3),
        name="last",
    )(corr, key_proj, value_proj)


def mix_kernel(place_ref, grad_out_ref, *refs):
    near_w, far_w, passed = refs[:4], refs[4:8], refs[8:12]
    parts, near_out, far_out, weight, grad, sems, out_sems = refs[-7:]
    my_z, my_x, my_core, my_y = (place_ref[n] for n in range(4))
    width = weight.shape[3]
    copies = []

    def begin(source, target):
        copy = pltpu.make_async_copy(source, target, sems.at[len(copies)])
        copy.start()
        copies.append(copy)

    for back in range(4):
        for core in range(2):
            for s in range(1, 4):
                begin(
                    passed[back].at[s - 1, :, pl.ds(core * width, width)],
                    grad.at[lax.rem(my_y - back + 4, 4), core, lax.rem(my_z - s + 4, 4)],
                )
    for col in range(4):
        for core in range(2):
            start = pl.multiple_of(((my_z * 4 + col) * 2 + core) * width, width)
            begin(grad_out_ref.at[:, pl.ds(start, width)], grad.at[col, core, my_z])
    fixed = len(copies)
    step = 256
    for m in range(weight.shape[2] // step):
        here = pl.ds(m * step, step)
        for back in range(4):
            col = lax.rem(my_x - back + 4, 4)
            begin(near_w[back].at[here], weight.at[my_core, col, here])
            begin(far_w[back].at[here], weight.at[1 - my_core, col, here])
    for copy in copies[:fixed]:
        copy.wait()

    near_copy = pltpu.make_async_copy(grad.at[:, my_core], near_out, out_sems.at[0])
    far_copy = pltpu.make_async_copy(grad.at[:, 1 - my_core], far_out, out_sems.at[1])
    near_copy.start()
    far_copy.start()

    lines = [
        jnp.concatenate([grad[n // 2, n % 2, z] for n in range(8)], 1) for z in range(4)
    ]
    grad_rows = jnp.concatenate(lines, 0)
    for m in range(weight.shape[2] // step):
        for copy in copies[fixed + 8 * m : fixed + 8 * m + 8]:
            copy.wait()
        here = slice(m * step, (m + 1) * step)
        rows = jnp.concatenate([weight[n % 2, n // 2, here, :] for n in range(8)], 1)
        part = lax.dot_general(
            rows, grad_rows, (((1,), (1,)), ((), ())), preferred_element_type=f32
        )
        parts[here, :] = part.astype(bf16)
    near_copy.wait()
    far_copy.wait()


def mix_call(place, grad_out, near_w, far_w, passed):
    toks = grad_out.shape[0]
    rows, width = near_w[0].shape
    any_spec = pl.BlockSpec(memory_space=pl.ANY)
    vmem = pl.BlockSpec(memory_space=pltpu.VMEM)
    blocks = jax.ShapeDtypeStruct((4, 4, toks, width), bf16)
    return pl.pallas_call(
        mix_kernel,
        in_specs=[pl.BlockSpec(memory_space=pltpu.SMEM)] + [any_spec] * 13,
        out_specs=[vmem] + [any_spec] * 2,
        out_shape=[jax.ShapeDtypeStruct((rows, 4 * toks), bf16)] + [blocks] * 2,
        scratch_shapes=[
            pltpu.VMEM((2, 4, rows, width), bf16),
            pltpu.VMEM((4, 2, 4, toks, width), bf16),
            pltpu.SemaphoreType.DMA((64,)),
            pltpu.SemaphoreType.DMA((2,)),
        ],
        compiler_params=params(),
        cost_estimate=cost(2 * rows * toks * 4 * 8 * width, 9),
        name="mix",
    )(place, grad_out, *near_w, *far_w, *passed)


def product_kernel(extra, cols_ref, mixed_near, mixed_far, near, far, *refs):
    adds, outs = refs[:extra], refs[extra:]
    my_core = cols_ref[4]
    owners, owned, depth = mixed_near.shape
    half = depth // 2
    lines = [item[...].reshape(owners * owned, depth) for item in (mixed_near, mixed_far)]
    for n, out in enumerate(outs):
        col = cols_ref[n]
        own = near[col].reshape(half, near.shape[3])
        other = far[col].reshape(half, far.shape[3])
        columns = jnp.concatenate(
            [jnp.where(my_core == 0, own, other), jnp.where(my_core == 0, other, own)], 0
        )
        for core, rows in zip((my_core, 1 - my_core), lines):
            product = dot(rows, columns)
            product = product.reshape(owners, owned, product.shape[1])
            for item in adds:
                product = product + item[:, core].astype(f32)
            out[:, core] = product.astype(out.dtype)


def product_call(cols, mixed_near, mixed_far, near, far, adds, kinds):
    owners, owned, depth = mixed_near.shape
    width = near.shape[3]
    vmem = pl.BlockSpec(memory_space=pltpu.VMEM)
    return pl.pallas_call(
        functools.partial(product_kernel, len(adds)),
        in_specs=[pl.BlockSpec(memory_space=pltpu.SMEM)] + [vmem] * (4 + len(adds)),
        out_specs=[vmem] * len(kinds),
        out_shape=[jax.ShapeDtypeStruct((owners, 2, owned, width), kind) for kind in kinds],
        compiler_params=params(),
        cost_estimate=cost(4 * owners * owned * width * depth * len(kinds), 5),
        name="product",
    )(cols, mixed_near, mixed_far, near, far, *adds)


def shards(grad_out, out_weight, query_proj, key_proj, value_proj, filter_taps, skip_gain):
    tok_rows = grad_out.shape[0]
    context_size = lax.axis_size(CTX)
    seq_len = tok_rows * context_size
    group_width, width = out_weight.shape
    owned = group_width // context_size
    norm_scale = 1.0 / math.sqrt(seq_len)
    my_z, my_x, my_core, my_y = (lax.axis_index(name) for name in ("zh", "x", "core", "y"))
    table = jnp.asarray(tables(seq_len))
    order = (1, 3, 2)

    def shift(item, axis, by):
        size = lax.axis_size(axis)
        return lax.ppermute(item, axis, [(n, (n + by) % size) for n in range(size)])

    def swap(item):
        return shift(item, "core", 1)

    def to_all(item):
        return lax.all_to_all(item, CTX, split_axis=0, concat_axis=0, tiled=True)

    place = jnp.stack([my_z, my_x, my_core, my_y]).astype(jnp.int32)
    skip_rows = lax.dynamic_slice_in_dim(
        skip_gain, lax.axis_index(CTX) * owned, owned, 0
    )
    skip_rows = jnp.broadcast_to(skip_rows[:, None], (owned, tok_rows))

    def after(item, *others):
        return lax.optimization_barrier((item, *others))[0]

    packed = prep_call(key_proj, value_proj, filter_taps, query_proj, owned)
    fields = to_all(packed)
    grad_late, weight_late = after(grad_out, packed), after(out_weight, packed)

    passed, near_w = {}, {0: weight_late}
    for s in order:
        start = ((my_z + s) % 4 * 4 + my_y) * (2 * width)
        passed[s] = shift(lax.dynamic_slice_in_dim(grad_late, start, 2 * width, 1), "zh", s)
        if s != 2:
            near_w[s] = shift(weight_late, "x", s)
    held = lax.optimization_barrier((*(passed[s] for s in range(1, 4)), skip_rows))
    skip_rows = held[3]
    passed = {0: jnp.stack(held[:3])}
    near_w[2] = shift(after(out_weight, passed[0]), "x", 2)
    for s in order:
        passed[s] = shift(passed[0], "y", s)

    fields = after(fields, passed[0], near_w[1], near_w[3], skip_rows, place)
    total, spec, mixed = conv_call(fields, skip_rows, table)
    mixed = lax.all_to_all(
        mixed.reshape(16, owned, 8 * tok_rows), ("zh", "x"), split_axis=0, concat_axis=0, tiled=True
    )

    held = lax.optimization_barrier((*near_w.values(), *passed.values(), total))
    far_w = {s: swap(item) for s, item in zip(near_w, held)}
    far_w = [far_w[s] for s in range(4)]
    parts, near, far = mix_call(
        place, grad_out, [near_w[s] for s in range(4)], far_w, [passed[s] for s in range(4)]
    )
    far = swap(far)
    parts = to_all(parts.reshape(context_size, owned, 4 * tok_rows))
    mixed_far = swap(mixed)

    cols = [(my_x + s) % 4 for s in (2, 1, 3, 0)]
    near_cols = jnp.stack(cols + [my_core]).astype(jnp.int32)
    last_cols = jnp.stack(cols[3:] * 4 + [my_core]).astype(jnp.int32)
    sent = product_call(near_cols, mixed, mixed_far, near, far, (), (bf16,) * 3)
    sent = {s: shift(item, "x", s) for s, item in zip((2, 1, 3), sent)}
    parts = after(parts, sent[1], sent[3])
    corr = corr_call(parts, fields, total, spec, skip_rows, table)
    grad_weight = product_call(
        after(last_cols, corr), mixed, mixed_far, near, far, (sent[1], sent[3]), (f32,)
    )[0]
    corr = to_all(corr)
    grad_key, grad_value, grad_filter, grad_query = last_call(corr, key_proj, value_proj)
    grad_weight = grad_weight + sent[2].astype(f32)
    grad_weight = (grad_weight * norm_scale).astype(bf16).reshape(group_width, width)
    return (grad_query, grad_key, grad_value, grad_filter, grad_weight)


def solution(mesh):
    fine = Mesh(mesh.devices.reshape(4, 4, 2, 2, 4), CTX + TEN)
    rows_cols = P(CTX, TEN)
    in_specs = (P(CTX, None), P(TEN, CTX)) + (rows_cols,) * 4 + (P(TEN),)
    out_specs = (rows_cols,) * 4 + (P(TEN, CTX),)
    return jax.shard_map(
        shards, mesh=fine, in_specs=in_specs, out_specs=out_specs, check_vma=False
    )
```
